256 devices in a mesh: depth: 16 (over z, core), lat: 16 (over x, y).
Axes of the slice: x: 4, y: 4, z: 8, core: 2. Of those that a mesh axis runs over, the one named last changes fastest.
Arguments:
- volume: bfloat16 [256, 512, 2048], P('depth', 'lat'), may hold values from -6 to 6
- labels: int32 [256, 512, 2048], P('depth', 'lat'), may hold values from 0 to 7
- active_slices: int32 [16, 16], P('depth', 'lat'), may hold values from 0 to 16, as said below
- view_order: int32 [16], replicated, may hold values from 0 to 15, each once
- density_gain: float32 [8], replicated, may hold values from 0.5 to 3
- density_bias: float32 [8], replicated, may hold values from -2 to 1
- albedo_table: float32 [3, 8], replicated, may hold values from 0.1 to 1
- motion_table: float32 [2, 8], replicated, may hold values from -4 to 4
- conv_first: bfloat16 [3, 3, 32, 20], replicated, may hold values from -0.4375 to 0.4375
- bias_first: float32 [32], replicated, may hold values from -3 to 3
- conv_second: bfloat16 [3, 3, 3, 32], replicated, may hold values from -0.375 to 0.375
- bias_second: float32 [3], replicated, may hold values from -3 to 3
Outputs:
- aovs: float32 [20, 512, 2048], P(None, 'lat', 'depth')
- denoised: float32 [3, 512, 2048], P(None, 'lat', 'depth')
The draws below stay inside these ranges and needn't reach their ends.
Inputs may be any that keep to these rules, and one draw needn't show every extreme that they name: A brick has data only in its first active_slices[slab, band] slices; 0 marks an empty brick, and some brick is full. `view_order`: each slab appears once.
All inputs are finite; a program needn't handle non-finite values.
Results may differ from the reference program's by a relative error of at most 0.0031.
Values may be sent and summed in bfloat16 or wider, within the bound.
A program may use at most 128 MiB of HBM per device.

```python
import math
import jax
import jax.numpy as jnp
from jax import lax

SL = 16
RB = 32
W = 2048
CLASSES = 8
HID = 32
CH = 20
SLABS = 16
BANDS = 16
DEPTH_CELLS = 256
H = 512


def draw_active_slices(key, part):
    key = jax.random.fold_in(key, 11)
    first_key, second_key, third_key = jax.random.split(key, 3)
    base_counts = jax.random.randint(first_key, (SLABS, BANDS), 0, SL + 1)
    empty_marks = jax.random.randint(second_key, (SLABS, BANDS), 0, 4) == 0
    filled = jnp.where(empty_marks, 0, base_counts).reshape(-1)
    full_spot = jax.random.randint(third_key, (), 0, SLABS * BANDS)
    filled = jnp.where(jnp.arange(SLABS * BANDS) == full_spot, SL, filled)
    return filled.reshape(SLABS, BANDS).astype(jnp.int32)


def plant(drawn, own_key, low, top_value):
    longest = drawn.shape.index(max(drawn.shape))
    spots = []
    for shift in (0, 1):
        where = [jax.random.randint(jax.random.fold_in(own_key, axis), (), 0, length) for axis, length in enumerate(drawn.shape)]
        where[longest] = (where[longest] + shift) % drawn.shape[longest]
        spots.append(tuple(where))
    return drawn.at[spots[0]].set(low).at[spots[1]].set(top_value)


def shard_levels(rng, dims, cuts, low, largest):
    gain, own = 1.0, jax.random.fold_in(rng, 6)
    for dim, blocks in cuts:
        draws = jnp.exp(jax.random.uniform(jax.random.fold_in(own, dim), (blocks,), jnp.float32, low / len(cuts), largest / len(cuts)))
        gain = gain * jnp.repeat(draws, dims[dim] // blocks).reshape([-1 if axis == dim else 1 for axis in range(len(dims))])
    return gain


def gaussian(rng, shape, deviation, limit, shards=(), held_as=jnp.bfloat16):
    drawn = deviation * jax.random.normal(rng, shape, jnp.float32)
    if shards:
        drawn = drawn * shard_levels(rng, shape, shards, -0.22, 0.18)
    return jnp.clip(drawn, -limit, limit).astype(held_as)


def setup_inputs(seed: int = 0) -> dict:
    key_of = jax.random.split(jax.random.key(seed), 13)
    volume = gaussian(key_of[0], (DEPTH_CELLS, H, W), 1.0, 6.0, ((0, 16), (1, 16)))
    labels = plant(jax.random.randint(key_of[1], (DEPTH_CELLS, H, W), 0, CLASSES), jax.random.fold_in(key_of[1], 1), 0, CLASSES - 1).astype(jnp.int32)
    active_slices = draw_active_slices(jax.random.fold_in(key_of[12], 71), 0)
    view_order = jax.random.permutation(key_of[3], SLABS).astype(jnp.int32)
    density_gain = jnp.clip(jnp.exp(jax.random.uniform(key_of[4], (CLASSES,), jnp.float32, math.log(0.5), math.log(3.0))), 0.5, 3.0)
    density_bias = jnp.clip(jax.random.uniform(key_of[5], (CLASSES,), jnp.float32, -2.0, 1.0), -2.0, 1.0)
    albedo_table = jnp.clip(jax.random.uniform(key_of[6], (3, CLASSES), jnp.float32, 0.1, 1.0), 0.1, 1.0)
    motion_table = gaussian(key_of[7], (2, CLASSES), 1.0, 4.0, (), jnp.float32)
    conv_first = gaussian(key_of[8], (3, 3, HID, CH), (9 * CH) ** -0.5, 0.4375)
    bias_first = gaussian(key_of[9], (HID,), 0.5, 3.0, (), jnp.float32)
    conv_second = gaussian(key_of[10], (3, 3, 3, HID), (9 * HID) ** -0.5, 0.375)
    bias_second = gaussian(key_of[11], (3,), 0.5, 3.0, (), jnp.float32)
    return dict(volume=volume, labels=labels, active_slices=active_slices, view_order=view_order, density_gain=density_gain, density_bias=density_bias, albedo_table=albedo_table, motion_table=motion_table, conv_first=conv_first, bias_first=bias_first, conv_second=conv_second, bias_second=bias_second)


def render_plane(lower_plane, middle_plane, upper_plane, classes, active, offset, density_gain, density_bias, albedo_table, motion_table, optical):
    center = middle_plane[1:-1, 1:-1].astype(jnp.float32)
    below = lower_plane[1:-1, 1:-1].astype(jnp.float32)
    above = upper_plane[1:-1, 1:-1].astype(jnp.float32)
    grad_x = (middle_plane[1:-1, 2:].astype(jnp.float32) - middle_plane[1:-1, :-2].astype(jnp.float32)) * 0.5
    grad_y = (middle_plane[2:, 1:-1].astype(jnp.float32) - middle_plane[:-2, 1:-1].astype(jnp.float32)) * 0.5
    grad_z = (above - below) * 0.5
    inverse_norm = lax.rsqrt(grad_x * grad_x + grad_y * grad_y + grad_z * grad_z + 1.0)
    normal = jnp.stack([grad_x * inverse_norm, grad_y * inverse_norm, grad_z * inverse_norm], 0)
    class_count = density_gain.shape[0]
    onehot = (classes[None] == jnp.arange(class_count, dtype=jnp.int32)[:, None, None]).astype(jnp.float32)
    gain_map = lax.optimization_barrier(jnp.sum(density_gain[:, None, None] * onehot, 0))
    bias_map = lax.optimization_barrier(jnp.sum(density_bias[:, None, None] * onehot, 0))
    density = jax.nn.softplus(gain_map * center + bias_map)
    opacity = (1.0 - jnp.exp(-optical * density)) * active
    shading = 0.4 + 0.6 * jnp.maximum(0.48 * normal[0] + 0.6 * normal[1] + 0.64 * normal[2], 0.0)
    texture = 0.55 + 0.45 * jnp.tanh(below + above)
    albedo = lax.optimization_barrier(jnp.sum(albedo_table[:, :, None, None] * onehot[None], 1)) * texture[None]
    motion = lax.optimization_barrier(jnp.sum(motion_table[:, :, None, None] * onehot[None], 1)) * (1.0 + 0.5 * jnp.tanh(center))[None]
    feature = jnp.concatenate([albedo * shading[None], jnp.ones_like(center)[None], normal, albedo, onehot, motion], 0)
    contrib = opacity[None] * feature
    columns = contrib.shape[2]
    widened = jnp.pad(contrib, ((0, 0), (0, 0), (columns, 0)))
    return lax.dynamic_slice_in_dim(widened, (columns - offset).astype(jnp.int32), columns, 2)

def convolve(padded, weight):
    row_count = padded.shape[1] - 2
    col_count = padded.shape[2] - 2
    result = jnp.zeros((weight.shape[2], row_count, col_count), jnp.float32)
    for row_tap in range(3):
        for col_tap in range(3):
            window = padded[:, row_tap:row_tap + row_count, col_tap:col_tap + col_count]
            result = result + jnp.einsum('oc,crq->orq', weight[row_tap, col_tap], window, precision=lax.Precision.HIGHEST)
    return result

def reference(volume, labels, active_slices, view_order, density_gain, density_bias, albedo_table, motion_table, conv_first, bias_first, conv_second, bias_second):
    padded = jnp.pad(volume, 1)
    optical = 2.0 / DEPTH_CELLS
    channels = 12 + CLASSES
    band_of_row = jnp.arange(H, dtype=jnp.int32) // RB

    def slab_image(slab_index):
        band_counts = jnp.take(active_slices[slab_index], band_of_row)[:, None]

        def advance(slice_index, accum_state):
            depth_index = (slab_index * SL + slice_index).astype(jnp.int32)
            lower_plane = lax.dynamic_index_in_dim(padded, depth_index, 0, keepdims=False)
            middle_plane = lax.dynamic_index_in_dim(padded, depth_index + 1, 0, keepdims=False)
            upper_plane = lax.dynamic_index_in_dim(padded, depth_index + 2, 0, keepdims=False)
            classes = lax.dynamic_index_in_dim(labels, depth_index, 0, keepdims=False)
            active = (slice_index < band_counts).astype(jnp.float32)
            contrib = render_plane(lower_plane, middle_plane, upper_plane, classes, active, depth_index // 4, density_gain, density_bias, albedo_table, motion_table, optical)
            return accum_state + (1.0 - accum_state[3])[None] * contrib
        final = lax.fori_loop(0, SL, advance, jnp.zeros((channels, H, W), jnp.float32))
        return final.astype(jnp.bfloat16)
    stack = lax.map(slab_image, jnp.arange(SLABS, dtype=jnp.int32))

    def blend(rank, carry):
        composite, through = carry
        layer_piece = lax.dynamic_index_in_dim(stack, view_order[rank].astype(jnp.int32), 0, keepdims=False).astype(jnp.float32)
        composite = composite + through[None] * layer_piece
        through = through * (1.0 - layer_piece[3])
        return (composite, through)
    aovs, unused_through = lax.fori_loop(0, SLABS, blend, (jnp.zeros((channels, H, W), jnp.float32), jnp.ones((H, W), jnp.float32)))
    features = aovs.astype(jnp.bfloat16).astype(jnp.float32)
    feature_pad = jnp.pad(features, ((0, 0), (1, 1), (1, 1)))
    hidden = jnp.maximum(convolve(feature_pad, conv_first.astype(jnp.float32)) + bias_first[:, None, None], 0.0).astype(jnp.bfloat16)
    hidden_pad = jnp.pad(hidden.astype(jnp.float32), ((0, 0), (1, 1), (1, 1)))
    denoised = aovs[0:3] + convolve(hidden_pad, conv_second.astype(jnp.float32)) + bias_second[:, None, None]
    return (aovs, denoised)
```

```python
import jax
import jax.numpy as jnp
from jax import lax
from jax.experimental import pallas as pl
from jax.experimental.pallas import tpu as pltpu
from jax.sharding import PartitionSpec as P

MESH = pl.DeviceIdType.MESH
F32, BF16 = jnp.float32, jnp.bfloat16

SLICES = 16
ROWS = 32
COLS = 2048
LANES = 128
TILES = 16
BANDS = 16
CLASSES = 8
CHANNELS = 20
SLOTS = 24
HIDDEN = 32
GROUPS = 4
STEP = 4
WIDE = COLS + 2 * LANES
OPTICAL = 2.0 / 256
UNIT = 32000.0
MOTION_MAX = 6.0
OWN = 2 * SLOTS
OWN_END = OWN + ROWS * SLOTS
FEATS = 1024
GAIN, BIAS, ALBEDO, MOTION = 0, 1, 2, 5


def dot(a, b):
    return jnp.dot(a, b, preferred_element_type=F32)


def dot_first(a, b):
    return lax.dot_general(a, b, (((0,), (0,)), ((), ())), preferred_element_type=F32)


def dot_last(a, b):
    return lax.dot_general(a, b, (((1,), (1,)), ((), ())), preferred_element_type=F32)


def iota(shape, dim):
    return lax.broadcasted_iota(jnp.int32, shape, dim)


def hot(mask):
    return jnp.where(mask, 1.0, 0.0).astype(F32)


def lookup(table, index):
    return jnp.take_along_axis(table, index, axis=0, mode="promise_in_bounds")


def kernel(
    vol,
    lab,
    active,
    order,
    gain,
    bias,
    albedo,
    motion,
    conv_first,
    bias_first,
    conv_second,
    bias_second,
    aovs,
    denoised,
    volp,
    labi,
    labp,
    row_tmp,
    row_send,
    rowp,
    smat,
    kvec,
    tables,
    vs,
    gx,
    gy,
    tc,
    qs,
    alpha_send,
    alpha_recv,
    front,
    front_send,
    front_recv,
    part,
    chunk_send,
    chunk_recv,
    feat,
    edge,
    edge_recv,
    corner_recv,
    first_tmp,
    first_mat,
    second_tmp,
    second_mat,
    x_first,
    hidden,
    x_second,
    load_sem,
    halo_ssem,
    halo_rsem,
    alpha_ssem,
    alpha_rsem,
    front_ssem,
    front_rsem,
    chunk_ssem,
    chunk_rsem,
    rim_ssem,
    rim_rsem,
):
    me = lax.axis_index("depth")
    lat = lax.axis_index("lat")
    right = lax.rem(me + 1, TILES)
    left = lax.rem(me + TILES - 1, TILES)
    down = lax.rem(lat + 1, BANDS)
    up = lax.rem(lat + BANDS - 1, BANDS)
    not_first = hot(me > 0)
    not_last = hot(me < TILES - 1)
    not_top = hot(lat > 0)
    not_bottom = hot(lat < BANDS - 1)

    def remote(src, dst, ssem, rsem, device):
        return pltpu.make_async_remote_copy(
            src_ref=src,
            dst_ref=dst,
            send_sem=ssem,
            recv_sem=rsem,
            device_id=device,
            device_id_type=MESH,
        )

    load_vol = pltpu.make_async_copy(
        vol, volp.at[pl.ds(1, SLICES), :, pl.ds(LANES, COLS)], load_sem.at[0]
    )
    load_lab = pltpu.make_async_copy(lab, labi, load_sem.at[1])
    load_vol.start()
    load_lab.start()

    side = jnp.zeros((SLICES + 2, ROWS, LANES), BF16)
    volp[:, :, 0:LANES] = side
    volp[:, :, LANES + COLS :] = side
    labp[:, :, 0:LANES] = side[:SLICES]
    labp[:, :, LANES + COLS :] = side[:SLICES]
    rowp[:, :, 0:LANES] = side[0:2, 0:SLICES]
    rowp[:, :, LANES + COLS :] = side[0:2, 0:SLICES]
    feat[...] = jnp.zeros_like(feat)

    barrier = pltpu.get_barrier_semaphore()

    def greet(device):
        pl.semaphore_signal(barrier, inc=1, device_id=device, device_id_type=MESH)

    def greet_peer(i, carry):
        greet((lax.rem(me + i, TILES), lat))
        return carry

    lax.fori_loop(1, TILES, greet_peer, 0)
    for row in (up, down):
        for col in (left, me, right):
            greet((col, row))

    class_of = iota((CLASSES, LANES), 0)
    sources = (
        [(gain, None), (bias, None)]
        + [(albedo, c) for c in range(3)]
        + [(motion, c) for c in range(2)]
    )
    for number, (ref, row) in enumerate(sources):
        table = jnp.zeros((CLASSES, LANES), F32)
        for k in range(CLASSES):
            value = ref[k] if row is None else ref[row, k]
            table = jnp.where(class_of == k, value, table)
        tables[number] = table
    source_col = iota((3 * LANES, 2 * LANES), 0) - LANES
    target = iota((3 * LANES, 2 * LANES), 1)
    lane = lax.rem(target, LANES)
    for g in range(GROUPS):
        delta = source_col - lane + (STEP * me + g)
        smat[g] = jnp.where(
            target < LANES, hot(delta == 0), hot(delta == 1) - hot(delta == -1)
        ).astype(BF16)
    lane8 = iota((8, LANES), 1)
    for s in range(SLICES):
        factor = jnp.where(s < active[0, 0], -OPTICAL, 0.0).astype(F32)
        kvec[s, 1] = jnp.zeros((8, LANES), F32) + factor
        kvec[s, 0] = jnp.where(lane8 >= STEP * me + s // STEP, factor, 0.0)

    first_tmp[...] = jnp.zeros_like(first_tmp)
    second_tmp[...] = jnp.zeros_like(second_tmp)
    for dc in range(3):
        base = jnp.zeros((HIDDEN, 2 * LANES), F32)
        base2 = jnp.zeros((8, 3 * LANES), F32)
        for dr in range(3):
            first_tmp[:, 0:CHANNELS] = conv_first[dr, dc].astype(F32)
            wide = first_tmp[...]
            base = base + (pltpu.roll(wide, SLOTS * dr, 1) if dr else wide)
            second_tmp[0:3, 0:HIDDEN] = conv_second[dr, dc].astype(F32)
            wide = second_tmp[...]
            base2 = base2 + (pltpu.roll(wide, HIDDEN * dr, 1) if dr else wide)
        for i in range(8):
            moved = pltpu.roll(base, SLOTS * i, 1) if i else base
            first_mat[dc, i * HIDDEN : (i + 1) * HIDDEN, :] = moved.astype(BF16)
            moved = pltpu.roll(base2, HIDDEN * i, 1) if i else base2
            for c in range(3):
                second_mat[dc, c * 8 + i : c * 8 + i + 1, :] = moved[c : c + 1]

    load_vol.wait()
    pl.semaphore_wait(barrier, TILES - 1 + 6)

    inner = pl.ds(LANES, COLS)
    halo = [
        remote(
            volp.at[SLICES, :, inner],
            volp.at[0, :, inner],
            halo_ssem.at[0],
            halo_rsem.at[0],
            (right, lat),
        ),
        remote(
            volp.at[1, :, inner],
            volp.at[SLICES + 1, :, inner],
            halo_ssem.at[1],
            halo_rsem.at[1],
            (left, lat),
        ),
        remote(
            row_send.at[1],
            rowp.at[0, :, inner],
            halo_ssem.at[2],
            halo_rsem.at[2],
            (me, down),
        ),
        remote(
            row_send.at[0],
            rowp.at[1, :, inner],
            halo_ssem.at[3],
            halo_rsem.at[3],
            (me, up),
        ),
    ]
    halo[0].start()
    halo[1].start()
    for end in range(2):
        for s in range(SLICES):
            rows = volp[s + 1, 16 * end : 16 * end + 16, LANES : LANES + COLS].astype(F32)
            row_tmp[s : s + 1, :] = rows[15:16] if end else rows[0:1]
        row_send[end] = row_tmp[...].astype(BF16)
    halo[2].start()
    halo[3].start()

    load_lab.wait()

    def convert(s, carry):
        labp[s, :, LANES : LANES + COLS] = labi[s].astype(F32).astype(BF16)
        return carry

    lax.fori_loop(0, SLICES, convert, 0)

    def alpha_copy(j):
        return remote(
            alpha_send.at[j],
            alpha_recv.at[me],
            alpha_ssem.at[j],
            alpha_rsem.at[me],
            (j, lat),
        )

    def alpha_arrival(j):
        return remote(
            alpha_send.at[j],
            alpha_recv.at[j],
            alpha_ssem.at[j],
            alpha_rsem.at[j],
            (j, lat),
        )

    def window(j):
        return pl.ds(pl.multiple_of(j * LANES, LANES), 3 * LANES)

    def opacities(j, carry):
        through = [jnp.ones((8, LANES), F32) for _ in range(4)]
        edge_tile = jnp.minimum(j, 1)
        for g in range(GROUPS):
            first = STEP * g
            block = volp[1 + first : 1 + first + STEP, :, window(j)]
            moved = dot(block.reshape(STEP * ROWS, 3 * LANES), smat[g])
            block = labp[first : first + STEP, :, window(j)]
            classes = dot(block.reshape(STEP * ROWS, 3 * LANES), smat[g, :, 0:LANES])
            classes = classes.astype(jnp.int32)
            vs[j, g, 1 : 1 + STEP] = moved[:, :LANES].reshape(STEP, ROWS, LANES)
            gx[j, first : first + STEP] = moved[:, LANES:].reshape(STEP, ROWS, LANES)
            qs[j, first : first + STEP] = classes.reshape(STEP, ROWS, LANES)
            for i in range(STEP):
                factor = kvec[first + i, edge_tile]
                for rb in range(4):
                    at = i * ROWS + rb * 8
                    q = classes[at : at + 8]
                    x = lookup(tables[GAIN], q) * moved[at : at + 8, :LANES]
                    x = x + lookup(tables[BIAS], q)
                    t = jnp.exp(factor * jnp.log(1.0 + jnp.exp(x)))
                    tc[j, first + i, rb * 8 : rb * 8 + 8] = t
                    through[rb] = through[rb] * t
        alpha_send[j] = (1.0 - jnp.concatenate(through, axis=0)).astype(BF16)

        @pl.when(j != me)
        def _():
            alpha_copy(j).start()

        return carry

    lax.fori_loop(0, TILES, opacities, 0)
    alpha_recv[me] = alpha_send[me]

    for copy in halo:
        copy.wait()

    def boundary(j, carry):
        for g in range(GROUPS):
            shift = smat[g, :, 0:LANES]
            below = dot(volp[STEP * g, :, window(j)], shift)
            above = dot(volp[STEP * g + STEP + 1, :, window(j)], shift)
            vs[j, g, 0] = below * not_first if g == 0 else below
            vs[j, g, STEP + 1] = above * not_last if g == GROUPS - 1 else above
            over = dot(rowp[0, :, window(j)], shift) * not_top
            under = dot(rowp[1, :, window(j)], shift) * not_bottom
            for i in range(STEP):
                s = STEP * g + i
                center = vs[j, g, 1 + i]
                before = jnp.concatenate([over[s : s + 1], center[:-1]], axis=0)
                after = jnp.concatenate([center[1:], under[s : s + 1]], axis=0)
                gy[j, s] = after - before
        return carry

    lax.fori_loop(0, TILES, boundary, 0)

    def wait_alpha(i, carry):
        alpha_arrival(lax.rem(me + i, TILES)).wait_recv()
        return carry

    lax.fori_loop(1, TILES, wait_alpha, 0)
    run = jnp.ones((ROWS, LANES), F32)
    for j in range(TILES):
        front[j] = run
        run = run * (1.0 - alpha_recv[order[j]].astype(F32))

    def front_copy(k):
        return remote(
            front_send.at[k],
            front_recv.at[me],
            front_ssem.at[k],
            front_rsem.at[me],
            (k, lat),
        )

    def front_arrival(k):
        return remote(
            front_send.at[k],
            front_recv.at[k],
            front_ssem.at[k],
            front_rsem.at[k],
            (k, lat),
        )

    def send_front(k, carry):
        rank = jnp.int32(0)
        for j in range(TILES):
            rank = jnp.where(order[j] == k, j, rank)
        front_send[k] = jnp.round(front[rank] * UNIT).astype(jnp.int32).astype(jnp.int16)

        @pl.when(k != me)
        def _():
            front_copy(k).start()

        return carry

    lax.fori_loop(0, TILES, send_front, 0)
    front_recv[me] = front_send[me]

    def chunk_copy(i, device):
        return remote(
            chunk_send.at[i],
            chunk_recv.at[i],
            chunk_ssem.at[i],
            chunk_rsem.at[i],
            (device, lat),
        )

    def render(tile, rb):
        r0 = pl.ds(pl.multiple_of(rb * 8, 8), 8)
        zero = jnp.zeros((8, LANES), F32)
        state = [zero] * 19
        through = zero + 1.0
        for s in range(SLICES):
            g, i = s // STEP, s % STEP
            v = vs[tile, g, i + 1, r0]
            below = vs[tile, g, i, r0]
            above = vs[tile, g, i + 2, r0]
            dx = gx[tile, s, r0]
            dy = gy[tile, s, r0]
            q = qs[tile, s, r0]
            dz = above - below
            inverse = lax.rsqrt(dx * dx + dy * dy + dz * dz + 4.0)
            later = through * tc[tile, s, r0]
            w = through - later
            through = later
            wn = w * inverse
            light = 0.288 * dx + 0.36 * dy + 0.384 * dz
            shaded = 0.4 * w + wn * jnp.maximum(light, 0.0)
            texture = 0.55 + 0.45 * jnp.tanh(below + above)
            plain = w * texture
            color = shaded * texture
            moving = w + (0.5 * w) * jnp.tanh(v)
            new = []
            tints = [lookup(tables[ALBEDO + c], q) for c in range(3)]
            new += [tint * color for tint in tints]
            new += [wn * dx, wn * dy, wn * dz]
            new += [tint * plain for tint in tints]
            new += [jnp.where(q == k, w, 0.0) for k in range(CLASSES - 1)]
            new += [lookup(tables[MOTION + c], q) * moving for c in range(2)]
            state = [a + b for a, b in zip(state, new)] + state[len(new) :]
        opacity = 1.0 - through
        covered = state[9:16]
        last = opacity - sum(covered[1:], covered[0])
        final = state[0:3] + [opacity] + state[3:9] + covered + [last] + state[16:18]
        for c in range(CHANNELS):
            part[c, r0] = final[c]

    def codes(tile):
        scale = front_recv[tile].astype(jnp.int32).astype(F32)[None]
        image = part[...].astype(BF16).astype(F32)
        units = jnp.concatenate(
            [image[0:18] * scale, image[18:CHANNELS] * (scale * (1.0 / MOTION_MAX))], axis=0
        )
        return jnp.round(units).astype(jnp.int32)

    def tile_step(i, carry):
        half = i // 2
        odd = lax.rem(i, 2)
        distance = jnp.where(odd == 0, 8 - half, half - 7)
        tile = lax.rem(me + distance + TILES, TILES)

        def row_block(rb, inner_carry):
            render(tile, rb)
            return inner_carry

        lax.fori_loop(0, 4, row_block, 0)

        @pl.when(i == 0)
        def _():
            def wait_front(k, inner_carry):
                front_arrival(lax.rem(me + k, TILES)).wait_recv()
                return inner_carry

            lax.fori_loop(1, TILES, wait_front, 0)

        @pl.when(i < 2)
        def _():
            chunk_send[i] = codes(tile).astype(jnp.int16)

        @pl.when((i >= 2) & (i < TILES - 1))
        def _():
            chunk_copy(i - 2, right).wait_recv()
            total = codes(tile) + chunk_recv[i - 2].astype(jnp.int32)
            chunk_send[i] = total.astype(jnp.int16)

        @pl.when(i < TILES - 1)
        def _():
            chunk_copy(i, jnp.where(odd == 0, right, left)).start()

        return carry

    lax.fori_loop(0, TILES, tile_step, 0)
    chunk_copy(TILES - 3, right).wait_recv()
    chunk_copy(TILES - 2, right).wait_recv()
    summed = chunk_recv[TILES - 3].astype(jnp.int32) + chunk_recv[TILES - 2].astype(jnp.int32)
    scale = front_recv[me].astype(jnp.int32).astype(F32)[None]
    composite = part[...].astype(BF16).astype(F32) * (scale * (1.0 / UNIT)) + jnp.concatenate(
        [
            summed[0:18].astype(F32) * (1.0 / UNIT),
            summed[18:CHANNELS].astype(F32) * (MOTION_MAX / UNIT),
        ],
        axis=0,
    )
    aovs[...] = composite
    rounded = composite.astype(BF16).astype(F32)
    for c in range(CHANNELS):
        for rb in range(4):
            start = OWN + rb * 8 * SLOTS + c
            feat[pl.ds(start, 8, stride=SLOTS), :] = rounded[c, rb * 8 : rb * 8 + 8]

    pick = iota((8, LANES), 0)
    at = iota((8, LANES), 1)
    chosen = (
        ((pick == 0) & (at == LANES - 2))
        | ((pick == 1) & (at == LANES - 1))
        | ((pick == 2) & (at == 0))
        | ((pick == 3) & (at == 1))
    )
    rim = [
        remote(
            feat.at[pl.ds(OWN, OWN)],
            feat.at[pl.ds(OWN_END, OWN)],
            rim_ssem.at[0],
            rim_rsem.at[0],
            (me, up),
        ),
        remote(
            feat.at[pl.ds(OWN_END - OWN, OWN)],
            feat.at[pl.ds(0, OWN)],
            rim_ssem.at[1],
            rim_rsem.at[1],
            (me, down),
        ),
    ]
    rim[0].start()
    rim[1].start()
    edge[...] = dot_last(hot(chosen).astype(BF16), feat[OWN:OWN_END].astype(BF16))
    top = pl.ds(0, LANES)
    bottom = pl.ds(ROWS * SLOTS - LANES, LANES)
    targets = [
        (edge, edge_recv.at[0], (right, lat)),
        (edge, edge_recv.at[1], (left, lat)),
        (edge.at[:, top], corner_recv.at[0], (right, up)),
        (edge.at[:, top], corner_recv.at[1], (left, up)),
        (edge.at[:, bottom], corner_recv.at[2], (right, down)),
        (edge.at[:, bottom], corner_recv.at[3], (left, down)),
    ]
    for number, (src, dst, device) in enumerate(targets):
        copy = remote(src, dst, rim_ssem.at[2 + number], rim_rsem.at[2 + number], device)
        copy.start()
        rim.append(copy)

    n = iota((1, 6 * LANES), 1)
    tap = n // (2 * LANES) - 1
    spot = lax.rem(n, 2 * LANES)
    column = jnp.where(
        spot < LANES,
        spot + tap,
        jnp.where(
            spot == LANES, tap - 1, jnp.where(spot == LANES + 1, LANES + tap, -9)
        ),
    )
    own_shift = hot(iota((LANES, 6 * LANES), 0) == column).astype(BF16)
    k16 = iota((16, 6 * LANES), 0)
    wanted = jnp.where(
        k16 < 2, k16 - 2, jnp.where((k16 == 10) | (k16 == 11), k16 + LANES - 10, -99)
    )
    rim_shift = hot(wanted == column).astype(BF16)
    for copy in rim:
        copy.wait()

    def both(first, second):
        return jnp.concatenate([first * not_first, second * not_last], axis=0).astype(BF16)

    middle = dot_first(both(edge_recv[0], edge_recv[1]), rim_shift)
    lower = dot_first(both(corner_recv[0], corner_recv[1]), rim_shift)
    upper = dot_first(both(corner_recv[2], corner_recv[3]), rim_shift)
    own = dot(feat[...].astype(BF16), own_shift)
    pieces = [
        (0, (own[0:OWN] + upper[LANES - OWN :]) * not_top),
        (OWN, own[OWN:OWN_END] + middle),
        (OWN_END, (own[OWN_END : OWN_END + OWN] + lower[0:OWN]) * not_bottom),
        (OWN_END + OWN, own[OWN_END + OWN :]),
    ]
    for start, piece in pieces:
        for dc in range(3):
            x_first[dc, start : start + piece.shape[0], :] = piece[
                :, dc * 2 * LANES : (dc + 1) * 2 * LANES
            ].astype(BF16)

    eye = iota((HIDDEN, HIDDEN), 0) == iota((HIDDEN, HIDDEN), 1)
    bias_col = jnp.sum(jnp.where(eye, bias_first[...], 0.0), axis=1, keepdims=True)
    bias_all = jnp.concatenate([bias_col] * 8, axis=0)
    spot = iota((1, 2 * LANES), 1)
    inside = jnp.where(
        spot == LANES, not_first, jnp.where(spot == LANES + 1, not_last, 1.0)
    )
    row_of = iota((8 * HIDDEN, 1), 0) // HIDDEN
    for b in range(5):
        total = jnp.zeros((8 * HIDDEN, 2 * LANES), F32)
        for dc in range(3):
            x = x_first[dc, 8 * SLOTS * b : 8 * SLOTS * b + 2 * LANES, :]
            total = total + dot(first_mat[dc], x)
        total = jnp.maximum(total + bias_all, 0.0) * inside
        if b == 0:
            total = total * jnp.where(row_of == 0, not_top, 1.0)
        if b == 4:
            total = total * jnp.where(row_of == 1, not_bottom, 1.0)
        hidden[8 * HIDDEN * b : 8 * HIDDEN * (b + 1), :] = total.astype(BF16)

    n = iota((1, 3 * LANES), 1)
    column = lax.rem(n, LANES) + n // LANES - 1
    source = jnp.where(column < 0, LANES, jnp.where(column == LANES, LANES + 1, column))
    second_shift = hot(iota((2 * LANES, 3 * LANES), 0) == source).astype(BF16)
    moved = dot(hidden[...], second_shift)
    for dc in range(3):
        x_second[dc] = moved[:, dc * LANES : (dc + 1) * LANES].astype(BF16)
    for b in range(4):
        total = jnp.zeros((3 * 8, LANES), F32)
        for dc in range(3):
            x = x_second[dc, 8 * HIDDEN * b : 8 * HIDDEN * b + 10 * HIDDEN, :]
            total = total + dot(second_mat[dc][:, 0 : 10 * HIDDEN].astype(BF16), x)
        for c in range(3):
            rows = slice(8 * b, 8 * b + 8)
            color = aovs[c, rows] + total[8 * c : 8 * c + 8]
            denoised[c, rows] = color + bias_second[c]

    def sent(k, carry):
        other = lax.rem(me + k, TILES)
        alpha_copy(other).wait_send()
        front_copy(other).wait_send()
        chunk_copy(k - 1, right).wait_send()
        return carry

    lax.fori_loop(1, TILES, sent, 0)


def per_device(
    volume,
    labels,
    active_slices,
    view_order,
    density_gain,
    density_bias,
    albedo_table,
    motion_table,
    conv_first,
    bias_first,
    conv_second,
    bias_second,
):
    smem = pl.BlockSpec(memory_space=pltpu.SMEM)
    vmem = pl.BlockSpec(memory_space=pltpu.VMEM)
    anywhere = pl.BlockSpec(memory_space=pl.ANY)
    cells = (TILES, SLICES, ROWS, LANES)
    tile = (TILES, ROWS, LANES)
    chunk = (CHANNELS, ROWS, LANES)
    dma = pltpu.SemaphoreType.DMA
    return pl.pallas_call(
        kernel,
        out_shape=(
            jax.ShapeDtypeStruct(chunk, F32),
            jax.ShapeDtypeStruct((3, ROWS, LANES), F32),
        ),
        in_specs=[anywhere, anywhere] + [smem] * 6 + [vmem] * 3 + [smem],
        out_specs=(vmem, vmem),
        scratch_shapes=[
            pltpu.VMEM((SLICES + 2, ROWS, WIDE), BF16),
            pltpu.VMEM((SLICES, ROWS, COLS), jnp.int32),
            pltpu.VMEM((SLICES, ROWS, WIDE), BF16),
            pltpu.VMEM((SLICES, COLS), F32),
            pltpu.VMEM((2, SLICES, COLS), BF16),
            pltpu.VMEM((2, SLICES, WIDE), BF16),
            pltpu.VMEM((GROUPS, 3 * LANES, 2 * LANES), BF16),
            pltpu.VMEM((SLICES, 2, 8, LANES), F32),
            pltpu.VMEM((7, CLASSES, LANES), F32),
            pltpu.VMEM((TILES, GROUPS, STEP + 2, ROWS, LANES), F32),
            pltpu.VMEM(cells, F32),
            pltpu.VMEM(cells, F32),
            pltpu.VMEM(cells, F32),
            pltpu.VMEM(cells, jnp.int32),
            pltpu.VMEM(tile, BF16),
            pltpu.VMEM(tile, BF16),
            pltpu.VMEM(tile, F32),
            pltpu.VMEM(tile, jnp.int16),
            pltpu.VMEM(tile, jnp.int16),
            pltpu.VMEM(chunk, F32),
            pltpu.VMEM((TILES - 1,) + chunk, jnp.int16),
            pltpu.VMEM((TILES - 1,) + chunk, jnp.int16),
            pltpu.VMEM((FEATS, LANES), F32),
            pltpu.VMEM((8, ROWS * SLOTS), F32),
            pltpu.VMEM((2, 8, ROWS * SLOTS), F32),
            pltpu.VMEM((4, 8, LANES), F32),
            pltpu.VMEM((HIDDEN, 2 * LANES), F32),
            pltpu.VMEM((3, 8 * HIDDEN, 2 * LANES), BF16),
            pltpu.VMEM((8, 3 * LANES), F32),
            pltpu.VMEM((3, 24, 3 * LANES), F32),
            pltpu.VMEM((3, FEATS, 2 * LANES), BF16),
            pltpu.VMEM((40 * HIDDEN, 2 * LANES), BF16),
            pltpu.VMEM((3, 40 * HIDDEN, LANES), BF16),
            dma((2,)),
            dma((4,)),
            dma((4,)),
            dma((TILES,)),
            dma((TILES,)),
            dma((TILES,)),
            dma((TILES,)),
            dma((TILES - 1,)),
            dma((TILES - 1,)),
            dma((8,)),
            dma((8,)),
        ],
        compiler_params=pltpu.CompilerParams(
            collective_id=0, has_side_effects=True, vmem_limit_bytes=60 * 1024 * 1024
        ),
    )(
        volume,
        labels,
        active_slices,
        view_order,
        density_gain,
        density_bias,
        albedo_table,
        motion_table,
        conv_first,
        bias_first.reshape(1, HIDDEN),
        conv_second,
        bias_second,
    )


def solution(mesh):
    placed = (P("depth", "lat", None),) * 2 + (P("depth", "lat"),) + (P(),) * 9
    return jax.shard_map(
        per_device,
        mesh=mesh,
        in_specs=placed,
        out_specs=(P(None, "lat", "depth"), P(None, "lat", "depth")),
        check_vma=False,
    )
```

```python
import jax
import jax.numpy as jnp
from jax import lax
from jax.experimental import pallas as pl
from jax.experimental.pallas import tpu as pltpu
from jax.sharding import PartitionSpec as P

MESH = pl.DeviceIdType.MESH
F32, BF16 = jnp.float32, jnp.bfloat16

SLICES = 16
ROWS = 32
COLS = 2048
LANES = 128
TILES = 16
BANDS = 16
CLASSES = 8
CHANNELS = 20
SLOTS = 24
HIDDEN = 32
GROUPS = 4
STEP = 4
WIDE = COLS + 2 * LANES
OPTICAL = 2.0 / 256
UNIT = 32000.0
MOTION_MAX = 6.0
HALF = 16
BODY = slice(8, 8 + ROWS)
OWN = 2 * SLOTS
OWN_END = OWN + ROWS * SLOTS
FEATS = 1024
GAIN, BIAS, ALBEDO, MOTION = 0, 1, 2, 5


def dot(a, b):
    return jnp.dot(a, b, preferred_element_type=F32)


def dot_first(a, b):
    return lax.dot_general(a, b, (((0,), (0,)), ((), ())), preferred_element_type=F32)


def dot_last(a, b):
    return lax.dot_general(a, b, (((1,), (1,)), ((), ())), preferred_element_type=F32)


def iota(shape, dim):
    return lax.broadcasted_iota(jnp.int32, shape, dim)


def hot(mask):
    return jnp.where(mask, 1.0, 0.0).astype(F32)


def lookup(table, index):
    return jnp.take_along_axis(table, index, axis=0, mode="promise_in_bounds")


def kernel(
    vol,
    lab,
    active,
    order,
    gain,
    bias,
    albedo,
    motion,
    conv_first,
    bias_first,
    conv_second,
    bias_second,
    aovs,
    denoised,
    volp,
    labi,
    labp,
    row_tmp,
    row_send,
    rowp,
    smat,
    kvec,
    tables,
    vs,
    gx,
    tc,
    qs,
    alpha_send,
    alpha_recv,
    front,
    front_send,
    front_recv,
    part,
    chunk_send,
    chunk_recv,
    feat,
    edge,
    edge_recv,
    corner_recv,
    first_tmp,
    first_mat,
    second_tmp,
    second_mat,
    x_first,
    hidden,
    x_second,
    own_shift,
    rim_shift,
    second_shift,
    load_sem,
    halo_ssem,
    halo_rsem,
    alpha_ssem,
    alpha_rsem,
    front_ssem,
    front_rsem,
    chunk_ssem,
    chunk_rsem,
    rim_ssem,
    rim_rsem,
):
    me = lax.axis_index("depth")
    lat = lax.axis_index("lat")
    right = lax.rem(me + 1, TILES)
    left = lax.rem(me + TILES - 1, TILES)
    down = lax.rem(lat + 1, BANDS)
    up = lax.rem(lat + BANDS - 1, BANDS)
    not_first = hot(me > 0)
    not_last = hot(me < TILES - 1)
    not_top = hot(lat > 0)
    not_bottom = hot(lat < BANDS - 1)

    def remote(src, dst, ssem, rsem, device):
        return pltpu.make_async_remote_copy(
            src_ref=src,
            dst_ref=dst,
            send_sem=ssem,
            recv_sem=rsem,
            device_id=device,
            device_id_type=MESH,
        )

    load_vol = pltpu.make_async_copy(
        vol, volp.at[pl.ds(1, SLICES), :, pl.ds(LANES, COLS)], load_sem.at[0]
    )
    load_lab = pltpu.make_async_copy(lab, labi, load_sem.at[1])
    load_vol.start()
    load_lab.start()

    side = jnp.zeros((SLICES + 2, ROWS, LANES), BF16)
    volp[:, :, 0:LANES] = side
    volp[:, :, LANES + COLS :] = side
    labp[:, :, 0:LANES] = side[:SLICES]
    labp[:, :, LANES + COLS :] = side[:SLICES]
    rowp[:, :, 0:LANES] = side[0:2, 0:SLICES]
    rowp[:, :, LANES + COLS :] = side[0:2, 0:SLICES]
    feat[...] = jnp.zeros_like(feat)

    barrier = pltpu.get_barrier_semaphore()

    def greet(device):
        pl.semaphore_signal(barrier, inc=1, device_id=device, device_id_type=MESH)

    def greet_peer(i, carry):
        greet((lax.rem(me + i, TILES), lat))
        return carry

    lax.fori_loop(1, TILES, greet_peer, 0)
    for row in (up, down):
        for col in (left, me, right):
            greet((col, row))

    class_of = iota((CLASSES, LANES), 0)
    sources = (
        [(gain, None), (bias, None)]
        + [(albedo, c) for c in range(3)]
        + [(motion, c) for c in range(2)]
    )
    for number, (ref, row) in enumerate(sources):
        table = jnp.zeros((CLASSES, LANES), F32)
        for k in range(CLASSES):
            value = ref[k] if row is None else ref[row, k]
            table = jnp.where(class_of == k, value, table)
        tables[number] = table
    source_col = iota((3 * LANES, 2 * LANES), 0) - LANES
    target = iota((3 * LANES, 2 * LANES), 1)
    lane = lax.rem(target, LANES)
    for g in range(GROUPS):
        delta = source_col - lane + (STEP * me + g)
        smat[g] = jnp.where(
            target < LANES, hot(delta == 0), hot(delta == 1) - hot(delta == -1)
        ).astype(BF16)
    lane8 = iota((8, LANES), 1)
    for s in range(SLICES):
        factor = jnp.where(s < active[0, 0], -OPTICAL, 0.0).astype(F32)
        kvec[s, 1] = jnp.zeros((8, LANES), F32) + factor
        kvec[s, 0] = jnp.where(lane8 >= STEP * me + s // STEP, factor, 0.0)

    load_vol.wait()
    pl.semaphore_wait(barrier, TILES - 1 + 6)

    inner = pl.ds(LANES, COLS)
    halo = [
        remote(
            volp.at[SLICES, :, inner],
            volp.at[0, :, inner],
            halo_ssem.at[0],
            halo_rsem.at[0],
            (right, lat),
        ),
        remote(
            volp.at[1, :, inner],
            volp.at[SLICES + 1, :, inner],
            halo_ssem.at[1],
            halo_rsem.at[1],
            (left, lat),
        ),
        remote(
            row_send.at[1],
            rowp.at[0, :, inner],
            halo_ssem.at[2],
            halo_rsem.at[2],
            (me, down),
        ),
        remote(
            row_send.at[0],
            rowp.at[1, :, inner],
            halo_ssem.at[3],
            halo_rsem.at[3],
            (me, up),
        ),
    ]
    halo[0].start()
    halo[1].start()
    for end in range(2):
        for s in range(SLICES):
            rows = volp[s + 1, 16 * end : 16 * end + 16, LANES : LANES + COLS].astype(F32)
            row_tmp[s : s + 1, :] = rows[15:16] if end else rows[0:1]
        row_send[end] = row_tmp[...].astype(BF16)
    halo[2].start()
    halo[3].start()

    load_lab.wait()

    def convert(s, carry):
        labp[s, :, LANES : LANES + COLS] = labi[s].astype(F32).astype(BF16)
        return carry

    lax.fori_loop(0, SLICES, convert, 0)

    def alpha_copy(j):
        return remote(
            alpha_send.at[j],
            alpha_recv.at[me],
            alpha_ssem.at[j],
            alpha_rsem.at[me],
            (j, lat),
        )

    def alpha_arrival(j):
        return remote(
            alpha_send.at[j],
            alpha_recv.at[j],
            alpha_ssem.at[j],
            alpha_rsem.at[j],
            (j, lat),
        )

    def window(j):
        return pl.ds(pl.multiple_of(j * LANES, LANES), 3 * LANES)

    def opacities(j, carry):
        through = [jnp.ones((8, LANES), F32) for _ in range(4)]
        edge_tile = jnp.minimum(j, 1)
        for g in range(GROUPS):
            first = STEP * g
            block = volp[1 + first : 1 + first + STEP, :, window(j)]
            moved = dot(block.reshape(STEP * ROWS, 3 * LANES), smat[g])
            block = labp[first : first + STEP, :, window(j)]
            classes = dot(block.reshape(STEP * ROWS, 3 * LANES), smat[g, :, 0:LANES])
            classes = classes.astype(jnp.int32)
            vs[j, g, 1 : 1 + STEP, BODY] = moved[:, :LANES].reshape(STEP, ROWS, LANES)
            gx[j, first : first + STEP] = moved[:, LANES:].reshape(STEP, ROWS, LANES)
            qs[j, first : first + STEP] = classes.reshape(STEP, ROWS, LANES)
            for i in range(STEP):
                factor = kvec[first + i, edge_tile]
                for rb in range(4):
                    at = i * ROWS + rb * 8
                    q = classes[at : at + 8]
                    x = lookup(tables[GAIN], q) * moved[at : at + 8, :LANES]
                    x = x + lookup(tables[BIAS], q)
                    t = jnp.exp(factor * jnp.log(1.0 + jnp.exp(x)))
                    tc[j, first + i, rb * 8 : rb * 8 + 8] = t
                    through[rb] = through[rb] * t
        opaque = 1.0 - jnp.concatenate(through, axis=0)
        alpha_send[j] = opaque.reshape(2, HALF, LANES).astype(BF16)

        @pl.when(j != me)
        def _():
            alpha_copy(j).start()

        return carry

    lax.fori_loop(0, TILES, opacities, 0)
    alpha_recv[me] = alpha_send[me]

    def boundary(j):
        for g in range(GROUPS):
            lines = [volp[STEP * g, :, window(j)], volp[STEP * g + STEP + 1, :, window(j)]]
            lines += [rowp[0, :, window(j)], rowp[1, :, window(j)]]
            moved = dot(jnp.concatenate(lines, axis=0), smat[g, :, 0:LANES])
            below, above = moved[0:ROWS], moved[ROWS : 2 * ROWS]
            vs[j, g, 0, BODY] = below * not_first if g == 0 else below
            vs[j, g, STEP + 1, BODY] = above * not_last if g == GROUPS - 1 else above
            over = moved[2 * ROWS : 2 * ROWS + SLICES] * not_top
            under = moved[2 * ROWS + SLICES :] * not_bottom
            for i in range(STEP):
                s = STEP * g + i
                vs[j, g, 1 + i, 7:8] = over[s : s + 1]
                vs[j, g, 1 + i, 8 + ROWS : 9 + ROWS] = under[s : s + 1]

    def wait_alpha(i, carry):
        alpha_arrival(lax.rem(me + i, TILES)).wait_recv()
        return carry

    def front_copy(k):
        return remote(
            front_send.at[k],
            front_recv.at[me],
            front_ssem.at[k],
            front_rsem.at[me],
            (k, lat),
        )

    def front_arrival(k):
        return remote(
            front_send.at[k],
            front_recv.at[k],
            front_ssem.at[k],
            front_rsem.at[k],
            (k, lat),
        )

    def send_front(k, carry):
        rank = jnp.int32(0)
        for j in range(TILES):
            rank = jnp.where(order[j] == k, j, rank)
        front_send[k] = jnp.round(front[rank] * UNIT).astype(jnp.int32).astype(jnp.int16)

        @pl.when(k != me)
        def _():
            front_copy(k).start()

        return carry

    def exchange_fronts():
        lax.fori_loop(1, TILES, wait_alpha, 0)
        run = jnp.ones((2, HALF, LANES), F32)
        for j in range(TILES):
            front[j] = run
            run = run * (1.0 - alpha_recv[order[j]].astype(F32))
        lax.fori_loop(0, TILES, send_front, 0)
        front_recv[me] = front_send[me]

    def chunk_copy(i, h, device):
        return remote(
            chunk_send.at[i, h],
            chunk_recv.at[i, h],
            chunk_ssem.at[i, h],
            chunk_rsem.at[i, h],
            (device, lat),
        )

    def render(tile, buffer, h, rb):
        first = h * HALF + rb * 8
        r0 = pl.ds(pl.multiple_of(first, 8), 8)
        here = pl.ds(pl.multiple_of(first + 8, 8), 8)
        zero = jnp.zeros((8, LANES), F32)
        state = [zero] * 19
        through = zero + 1.0
        for s in range(SLICES):
            g, i = s // STEP, s % STEP
            v = vs[tile, g, i + 1, here]
            below = vs[tile, g, i, here]
            above = vs[tile, g, i + 2, here]
            dx = gx[tile, s, r0]
            dy = vs[tile, g, i + 1, pl.ds(first + 9, 8)] - vs[tile, g, i + 1, pl.ds(first + 7, 8)]
            q = qs[tile, s, r0]
            dz = above - below
            inverse = lax.rsqrt(dx * dx + dy * dy + dz * dz + 4.0)
            later = through * tc[tile, s, r0]
            w = through - later
            through = later
            wn = w * inverse
            light = 0.288 * dx + 0.36 * dy + 0.384 * dz
            shaded = 0.4 * w + wn * jnp.maximum(light, 0.0)
            texture = 0.55 + 0.45 * jnp.tanh(below + above)
            plain = w * texture
            color = shaded * texture
            moving = w + (0.5 * w) * jnp.tanh(v)
            new = []
            tints = [lookup(tables[ALBEDO + c], q) for c in range(3)]
            new += [tint * color for tint in tints]
            new += [wn * dx, wn * dy, wn * dz]
            new += [tint * plain for tint in tints]
            new += [jnp.where(q == k, w, 0.0) for k in range(CLASSES - 1)]
            new += [lookup(tables[MOTION + c], q) * moving for c in range(2)]
            state = [a + b for a, b in zip(state, new)] + state[len(new) :]
        opacity = 1.0 - through
        covered = state[9:16]
        last = opacity - sum(covered[1:], covered[0])
        final = state[0:3] + [opacity] + state[3:9] + covered + [last] + state[16:18]
        for c in range(CHANNELS):
            part[buffer, h, c, pl.ds(pl.multiple_of(rb * 8, 8), 8)] = final[c]

    def scaled(i, h, factor):
        image = part[lax.rem(i, 2), h].astype(BF16).astype(F32)
        scale = front_recv[tile_of(i), h].astype(jnp.int32).astype(F32)[None] * factor
        return jnp.concatenate(
            [image[0:18] * scale, image[18:CHANNELS] * (scale * (1.0 / MOTION_MAX))], axis=0
        )

    def tile_of(i):
        distance = jnp.where(lax.rem(i, 2) == 0, 8 - i // 2, i // 2 - 7)
        return lax.rem(me + distance + TILES, TILES)

    def onward(i, h):
        @pl.when(i < 2)
        def _():
            chunk_send[i, h] = jnp.round(scaled(i, h, 1.0)).astype(jnp.int32).astype(jnp.int16)

        @pl.when(i >= 2)
        def _():
            own = jnp.round(scaled(i, h, 1.0)).astype(jnp.int32)
            chunk_copy(i - 2, h, right).wait_recv()
            total = own + chunk_recv[i - 2, h].astype(jnp.int32)
            chunk_send[i, h] = total.astype(jnp.int16)

        chunk_copy(i, h, jnp.where(lax.rem(i, 2) == 0, right, left)).start()

    def tile_step(i, carry):
        tile = tile_of(i)
        boundary(tile)

        def half_step(h, outer_carry):
            def row_block(rb, inner_carry):
                render(tile, lax.rem(i, 2), h, rb)
                return inner_carry

            lax.fori_loop(0, 2, row_block, 0)

            @pl.when((i == 1) & (h == 0))
            def _():
                def wait_front(k, inner_carry):
                    front_arrival(lax.rem(me + k, TILES)).wait_recv()
                    return inner_carry

                lax.fori_loop(1, TILES, wait_front, 0)
                onward(jnp.int32(0), jnp.int32(0))
                onward(jnp.int32(0), jnp.int32(1))

            @pl.when((i > 0) & (i < TILES - 1))
            def _():
                onward(i, h)

            return outer_carry

        lax.fori_loop(0, 2, half_step, 0)

        @pl.when(i == 0)
        def _():
            exchange_fronts()

        return carry

    for copy in halo:
        copy.wait()
    lax.fori_loop(0, TILES, tile_step, 0)

    turn = hot(iota((CHANNELS, CHANNELS), 0) == iota((CHANNELS, CHANNELS), 1)).astype(BF16)
    first_tmp[...] = jnp.zeros_like(first_tmp)
    second_tmp[...] = jnp.zeros_like(second_tmp)
    for dc in range(3):
        base = jnp.zeros((HIDDEN, 2 * LANES), F32)
        base2 = jnp.zeros((8, 3 * LANES), F32)
        for dr in range(3):
            first_tmp[:, 0:CHANNELS] = dot_first(conv_first[dr, dc], turn)
            wide = first_tmp[...]
            base = base + (pltpu.roll(wide, SLOTS * dr, 1) if dr else wide)
            second_tmp[0:3, 0:HIDDEN] = conv_second[dr, dc].astype(F32)
            wide = second_tmp[...]
            base2 = base2 + (pltpu.roll(wide, HIDDEN * dr, 1) if dr else wide)
        for i in range(8):
            moved = pltpu.roll(base, SLOTS * i, 1) if i else base
            first_mat[dc, i * HIDDEN : (i + 1) * HIDDEN, :] = moved.astype(BF16)
            moved = pltpu.roll(base2, HIDDEN * i, 1) if i else base2
            for c in range(3):
                second_mat[dc, c * 8 + i : c * 8 + i + 1, :] = moved[c : c + 1]

    n = iota((1, 6 * LANES), 1)
    tap = n // (2 * LANES) - 1
    spot = lax.rem(n, 2 * LANES)
    column = jnp.where(
        spot < LANES,
        spot + tap,
        jnp.where(
            spot == LANES, tap - 1, jnp.where(spot == LANES + 1, LANES + tap, -9)
        ),
    )
    own_shift[...] = hot(iota((LANES, 6 * LANES), 0) == column).astype(BF16)
    k16 = iota((16, 6 * LANES), 0)
    wanted = jnp.where(
        k16 < 2, k16 - 2, jnp.where((k16 == 10) | (k16 == 11), k16 + LANES - 10, -99)
    )
    rim_shift[...] = hot(wanted == column).astype(BF16)
    n = iota((1, 3 * LANES), 1)
    column = lax.rem(n, LANES) + n // LANES - 1
    source = jnp.where(column < 0, LANES, jnp.where(column == LANES, LANES + 1, column))
    second_shift[...] = hot(iota((2 * LANES, 3 * LANES), 0) == source).astype(BF16)
    x_first[:, OWN_END + OWN :, :] = jnp.zeros((3, FEATS - OWN_END - OWN, 2 * LANES), BF16)

    for h in range(2):
        chunk_copy(TILES - 3, h, right).wait_recv()
        chunk_copy(TILES - 2, h, right).wait_recv()
        summed = chunk_recv[TILES - 3, h].astype(jnp.int32)
        summed = summed + chunk_recv[TILES - 2, h].astype(jnp.int32)
        total = scaled(TILES - 1, h, 1.0) + summed.astype(F32)
        for c in range(CHANNELS):
            unit = (MOTION_MAX if c >= 18 else 1.0) / UNIT
            for rb in range(2):
                row = h * HALF + rb * 8
                block = total[c, rb * 8 : rb * 8 + 8] * unit
                aovs[c, row : row + 8] = block
                start = OWN + row * SLOTS + c
                feat[pl.ds(start, 8, stride=SLOTS), :] = block.astype(BF16).astype(F32)

    pick = iota((8, LANES), 0)
    at = iota((8, LANES), 1)
    chosen = (
        ((pick == 0) & (at == LANES - 2))
        | ((pick == 1) & (at == LANES - 1))
        | ((pick == 2) & (at == 0))
        | ((pick == 3) & (at == 1))
    )
    rim = [
        remote(
            feat.at[pl.ds(OWN, OWN)],
            feat.at[pl.ds(OWN_END, OWN)],
            rim_ssem.at[0],
            rim_rsem.at[0],
            (me, up),
        ),
        remote(
            feat.at[pl.ds(OWN_END - OWN, OWN)],
            feat.at[pl.ds(0, OWN)],
            rim_ssem.at[1],
            rim_rsem.at[1],
            (me, down),
        ),
    ]
    rim[0].start()
    rim[1].start()
    edge[...] = dot_last(hot(chosen).astype(BF16), feat[OWN:OWN_END].astype(BF16))
    top = pl.ds(0, LANES)
    bottom = pl.ds(ROWS * SLOTS - LANES, LANES)
    targets = [
        (edge, edge_recv.at[0], (right, lat)),
        (edge, edge_recv.at[1], (left, lat)),
        (edge.at[:, top], corner_recv.at[0], (right, up)),
        (edge.at[:, top], corner_recv.at[1], (left, up)),
        (edge.at[:, bottom], corner_recv.at[2], (right, down)),
        (edge.at[:, bottom], corner_recv.at[3], (left, down)),
    ]
    for number, (src, dst, device) in enumerate(targets):
        copy = remote(src, dst, rim_ssem.at[2 + number], rim_rsem.at[2 + number], device)
        copy.start()
        rim.append(copy)

    def put(start, end, values, add):
        for dc in range(3):
            for side in range(2):
                if add and dc == 1 and side == 0:
                    continue
                at = 2 * dc + side
                block = values[:, at * LANES : (at + 1) * LANES].astype(BF16)
                lanes = slice(side * LANES, (side + 1) * LANES)
                if add:
                    block = block + x_first[dc, start:end, lanes]
                x_first[dc, start:end, lanes] = block

    put(OWN, OWN_END, dot(feat[OWN:OWN_END].astype(BF16), own_shift[...]), False)
    for copy in rim:
        copy.wait()

    def both(first, second):
        return jnp.concatenate([first * not_first, second * not_last], axis=0).astype(BF16)

    put(OWN, OWN_END, dot_first(both(edge_recv[0], edge_recv[1]), rim_shift[...]), True)
    lower = dot_first(both(corner_recv[0], corner_recv[1]), rim_shift[...])
    upper = dot_first(both(corner_recv[2], corner_recv[3]), rim_shift[...])
    over = dot(feat[0:OWN].astype(BF16), own_shift[...])
    under = dot(feat[OWN_END : OWN_END + OWN].astype(BF16), own_shift[...])
    put(0, OWN, (over + upper[LANES - OWN :]) * not_top, False)
    put(OWN_END, OWN_END + OWN, (under + lower[0:OWN]) * not_bottom, False)

    eye = iota((HIDDEN, HIDDEN), 0) == iota((HIDDEN, HIDDEN), 1)
    bias_col = jnp.sum(jnp.where(eye, bias_first[...], 0.0), axis=1, keepdims=True)
    bias_all = jnp.concatenate([bias_col] * 8, axis=0)
    spot = iota((1, 2 * LANES), 1)
    inside = jnp.where(
        spot == LANES, not_first, jnp.where(spot == LANES + 1, not_last, 1.0)
    )
    row_of = iota((8 * HIDDEN, 1), 0) // HIDDEN
    for b in range(5):
        total = jnp.zeros((8 * HIDDEN, 2 * LANES), F32)
        for dc in range(3):
            x = x_first[dc, 8 * SLOTS * b : 8 * SLOTS * b + 2 * LANES, :]
            total = total + dot(first_mat[dc], x)
        total = jnp.maximum(total + bias_all, 0.0) * inside
        if b == 0:
            total = total * jnp.where(row_of == 0, not_top, 1.0)
        if b == 4:
            total = total * jnp.where(row_of == 1, not_bottom, 1.0)
        hidden[8 * HIDDEN * b : 8 * HIDDEN * (b + 1), :] = total.astype(BF16)

    moved = dot(hidden[...], second_shift[...])
    for dc in range(3):
        x_second[dc] = moved[:, dc * LANES : (dc + 1) * LANES].astype(BF16)
    for b in range(4):
        total = jnp.zeros((3 * 8, LANES), F32)
        for dc in range(3):
            x = x_second[dc, 8 * HIDDEN * b : 8 * HIDDEN * b + 10 * HIDDEN, :]
            total = total + dot(second_mat[dc][:, 0 : 10 * HIDDEN].astype(BF16), x)
        for c in range(3):
            rows = slice(8 * b, 8 * b + 8)
            color = aovs[c, rows] + total[8 * c : 8 * c + 8]
            denoised[c, rows] = color + bias_second[c]

    def sent(k, carry):
        other = lax.rem(me + k, TILES)
        alpha_copy(other).wait_send()
        front_copy(other).wait_send()
        chunk_copy(k - 1, 0, right).wait_send()
        chunk_copy(k - 1, 1, right).wait_send()
        return carry

    lax.fori_loop(1, TILES, sent, 0)


def per_device(
    volume,
    labels,
    active_slices,
    view_order,
    density_gain,
    density_bias,
    albedo_table,
    motion_table,
    conv_first,
    bias_first,
    conv_second,
    bias_second,
):
    smem = pl.BlockSpec(memory_space=pltpu.SMEM)
    vmem = pl.BlockSpec(memory_space=pltpu.VMEM)
    anywhere = pl.BlockSpec(memory_space=pl.ANY)
    cells = (TILES, SLICES, ROWS, LANES)
    tile = (TILES, 2, HALF, LANES)
    chunk = (CHANNELS, ROWS, LANES)
    pieces = (2, CHANNELS, HALF, LANES)
    dma = pltpu.SemaphoreType.DMA
    return pl.pallas_call(
        kernel,
        out_shape=(
            jax.ShapeDtypeStruct(chunk, F32),
            jax.ShapeDtypeStruct((3, ROWS, LANES), F32),
        ),
        in_specs=[anywhere, anywhere] + [smem] * 6 + [vmem] * 3 + [smem],
        out_specs=(vmem, vmem),
        scratch_shapes=[
            pltpu.VMEM((SLICES + 2, ROWS, WIDE), BF16),
            pltpu.VMEM((SLICES, ROWS, COLS), jnp.int32),
            pltpu.VMEM((SLICES, ROWS, WIDE), BF16),
            pltpu.VMEM((SLICES, COLS), F32),
            pltpu.VMEM((2, SLICES, COLS), BF16),
            pltpu.VMEM((2, SLICES, WIDE), BF16),
            pltpu.VMEM((GROUPS, 3 * LANES, 2 * LANES), BF16),
            pltpu.VMEM((SLICES, 2, 8, LANES), F32),
            pltpu.VMEM((7, CLASSES, LANES), F32),
            pltpu.VMEM((TILES, GROUPS, STEP + 2, ROWS + 16, LANES), F32),
            pltpu.VMEM(cells, F32),
            pltpu.VMEM(cells, F32),
            pltpu.VMEM(cells, jnp.int32),
            pltpu.VMEM(tile, BF16),
            pltpu.VMEM(tile, BF16),
            pltpu.VMEM(tile, F32),
            pltpu.VMEM(tile, jnp.int16),
            pltpu.VMEM(tile, jnp.int16),
            pltpu.VMEM((2,) + pieces, F32),
            pltpu.VMEM((TILES - 1,) + pieces, jnp.int16),
            pltpu.VMEM((TILES - 1,) + pieces, jnp.int16),
            pltpu.VMEM((FEATS, LANES), F32),
            pltpu.VMEM((8, ROWS * SLOTS), F32),
            pltpu.VMEM((2, 8, ROWS * SLOTS), F32),
            pltpu.VMEM((4, 8, LANES), F32),
            pltpu.VMEM((HIDDEN, 2 * LANES), F32),
            pltpu.VMEM((3, 8 * HIDDEN, 2 * LANES), BF16),
            pltpu.VMEM((8, 3 * LANES), F32),
            pltpu.VMEM((3, 24, 3 * LANES), F32),
            pltpu.VMEM((3, FEATS, 2 * LANES), BF16),
            pltpu.VMEM((40 * HIDDEN, 2 * LANES), BF16),
            pltpu.VMEM((3, 40 * HIDDEN, LANES), BF16),
            pltpu.VMEM((LANES, 6 * LANES), BF16),
            pltpu.VMEM((16, 6 * LANES), BF16),
            pltpu.VMEM((2 * LANES, 3 * LANES), BF16),
            dma((2,)),
            dma((4,)),
            dma((4,)),
            dma((TILES,)),
            dma((TILES,)),
            dma((TILES,)),
            dma((TILES,)),
            dma((TILES - 1, 2)),
            dma((TILES - 1, 2)),
            dma((8,)),
            dma((8,)),
        ],
        compiler_params=pltpu.CompilerParams(
            collective_id=0, has_side_effects=True, vmem_limit_bytes=60 * 1024 * 1024
        ),
    )(
        volume,
        labels,
        active_slices,
        view_order,
        density_gain,
        density_bias,
        albedo_table,
        motion_table,
        jnp.swapaxes(conv_first, 2, 3),
        bias_first.reshape(1, HIDDEN),
        conv_second,
        bias_second,
    )


def solution(mesh):
    placed = (P("depth", "lat", None),) * 2 + (P("depth", "lat"),) + (P(),) * 9
    return jax.shard_map(
        per_device,
        mesh=mesh,
        in_specs=placed,
        out_specs=(P(None, "lat", "depth"), P(None, "lat", "depth")),
        check_vma=False,
    )
```

```python
import jax
import jax.numpy as jnp
from jax import lax
from jax.experimental import pallas as pl
from jax.experimental.pallas import tpu as pltpu
from jax.sharding import PartitionSpec as P

MESH = pl.DeviceIdType.MESH
F32, BF16 = jnp.float32, jnp.bfloat16

SLICES = 16
ROWS = 32
COLS = 2048
LANES = 128
TILES = 16
BANDS = 16
CLASSES = 8
CHANNELS = 20
SLOTS = 24
HIDDEN = 32
GROUPS = 4
STEP = 4
WIDE = COLS + 2 * LANES
OPTICAL = 2.0 / 256
LOG2E = 1.4426950408889634
UNIT = 32000.0
MOTION_MAX = 8.0
CHIPS = TILES // 2
SENT = 18
GROUP = 18
PIECES = 2 * SENT // GROUP
FRONT_AT = 5
ONWARD_AT = {0: 5, 1: 5, 2: 9, 3: 9, 4: 13, 5: 13}
HALF = 16
BODY = slice(8, 8 + ROWS)
OWN = 2 * SLOTS
OWN_END = OWN + ROWS * SLOTS
FEATS = 1024
GAIN, BIAS, ALBEDO, MOTION = 0, 1, 2, 5


def dot(a, b):
    return jnp.dot(a, b, preferred_element_type=F32)


def dot_first(a, b):
    return lax.dot_general(a, b, (((0,), (0,)), ((), ())), preferred_element_type=F32)


def dot_last(a, b):
    return lax.dot_general(a, b, (((1,), (1,)), ((), ())), preferred_element_type=F32)


def iota(shape, dim):
    return lax.broadcasted_iota(jnp.int32, shape, dim)


def hot(mask):
    return jnp.where(mask, 1.0, 0.0).astype(F32)


def lookup(table, index):
    return jnp.take_along_axis(table, index, axis=0, mode="promise_in_bounds")


def kernel(
    vol,
    lab,
    active,
    order,
    gain,
    bias,
    albedo,
    motion,
    conv_first,
    bias_first,
    conv_second,
    bias_second,
    aovs,
    denoised,
    volp,
    labi,
    labp,
    row_tmp,
    row_send,
    rowp,
    smat,
    kvec,
    tables,
    vs,
    gx,
    tc,
    qs,
    alpha_send,
    alpha_recv,
    front,
    front_send,
    front_recv,
    part,
    opaque,
    pair_send,
    pair_recv,
    chunk_send,
    chunk_recv,
    feat,
    edge,
    edge_recv,
    corner_recv,
    first_tmp,
    first_mat,
    second_tmp,
    second_mat,
    x_first,
    hidden,
    x_second,
    own_shift,
    rim_shift,
    second_shift,
    load_sem,
    halo_ssem,
    halo_rsem,
    alpha_ssem,
    alpha_rsem,
    front_ssem,
    front_rsem,
    pair_ssem,
    pair_rsem,
    chunk_ssem,
    chunk_rsem,
    rim_ssem,
    rim_rsem,
):
    me = lax.axis_index("depth")
    lat = lax.axis_index("lat")
    core = lax.rem(me, 2)
    chip = me // 2
    sibling = me + 1 - 2 * core
    ahead = lax.rem(me + 2, TILES)
    behind = lax.rem(me + TILES - 2, TILES)
    right = lax.rem(me + 1, TILES)
    left = lax.rem(me + TILES - 1, TILES)
    down = lax.rem(lat + 1, BANDS)
    up = lax.rem(lat + BANDS - 1, BANDS)
    not_first = hot(me > 0)
    not_last = hot(me < TILES - 1)
    not_top = hot(lat > 0)
    not_bottom = hot(lat < BANDS - 1)

    def remote(src, dst, ssem, rsem, device):
        return pltpu.make_async_remote_copy(
            src_ref=src,
            dst_ref=dst,
            send_sem=ssem,
            recv_sem=rsem,
            device_id=device,
            device_id_type=MESH,
        )

    load_vol = pltpu.make_async_copy(
        vol, volp.at[pl.ds(1, SLICES), :, pl.ds(LANES, COLS)], load_sem.at[0]
    )
    load_lab = pltpu.make_async_copy(lab, labi, load_sem.at[1])
    load_vol.start()
    load_lab.start()

    side = jnp.zeros((SLICES + 2, ROWS, LANES), BF16)
    volp[:, :, 0:LANES] = side
    volp[:, :, LANES + COLS :] = side
    labp[:, :, 0:LANES] = side[:SLICES]
    labp[:, :, LANES + COLS :] = side[:SLICES]
    rowp[:, :, 0:LANES] = side[0:2, 0:SLICES]
    rowp[:, :, LANES + COLS :] = side[0:2, 0:SLICES]
    feat[...] = jnp.zeros_like(feat)

    barrier = pltpu.get_barrier_semaphore()

    def greet(device):
        pl.semaphore_signal(barrier, inc=1, device_id=device, device_id_type=MESH)

    def greet_peer(i, carry):
        greet((lax.rem(me + i, TILES), lat))
        return carry

    lax.fori_loop(1, TILES, greet_peer, 0)
    for row in (up, down):
        for col in (left, me, right):
            greet((col, row))

    class_of = iota((CLASSES, LANES), 0)
    sources = (
        [(gain, None), (bias, None)]
        + [(albedo, c) for c in range(3)]
        + [(motion, c) for c in range(2)]
    )
    for number, (ref, row) in enumerate(sources):
        table = jnp.zeros((CLASSES, LANES), F32)
        for k in range(CLASSES):
            value = ref[k] if row is None else ref[row, k]
            table = jnp.where(class_of == k, value, table)
        tables[number] = table * LOG2E if number < ALBEDO else table
    source_col = iota((3 * LANES, 2 * LANES), 0) - LANES
    target = iota((3 * LANES, 2 * LANES), 1)
    lane = lax.rem(target, LANES)
    for g in range(GROUPS):
        delta = source_col - lane + (STEP * me + g)
        smat[g] = jnp.where(
            target < LANES, hot(delta == 0), hot(delta == 1) - hot(delta == -1)
        ).astype(BF16)
    lane8 = iota((8, LANES), 1)
    for s in range(SLICES):
        factor = jnp.where(s < active[0, 0], -OPTICAL * LOG2E, 0.0).astype(F32)
        kvec[s, 1] = jnp.zeros((8, LANES), F32) + factor
        kvec[s, 0] = jnp.where(lane8 >= STEP * me + s // STEP, factor, 0.0)

    load_vol.wait()
    pl.semaphore_wait(barrier, TILES - 1 + 6)

    inner = pl.ds(LANES, COLS)
    halo = [
        remote(
            volp.at[SLICES, :, inner],
            volp.at[0, :, inner],
            halo_ssem.at[0],
            halo_rsem.at[0],
            (right, lat),
        ),
        remote(
            volp.at[1, :, inner],
            volp.at[SLICES + 1, :, inner],
            halo_ssem.at[1],
            halo_rsem.at[1],
            (left, lat),
        ),
        remote(
            row_send.at[1],
            rowp.at[0, :, inner],
            halo_ssem.at[2],
            halo_rsem.at[2],
            (me, down),
        ),
        remote(
            row_send.at[0],
            rowp.at[1, :, inner],
            halo_ssem.at[3],
            halo_rsem.at[3],
            (me, up),
        ),
    ]
    halo[0].start()
    halo[1].start()
    for end in range(2):
        for s in range(SLICES):
            rows = volp[s + 1, 16 * end : 16 * end + 16, LANES : LANES + COLS].astype(F32)
            row_tmp[s : s + 1, :] = rows[15:16] if end else rows[0:1]
        row_send[end] = row_tmp[...].astype(BF16)
    halo[2].start()
    halo[3].start()

    load_lab.wait()

    def convert(s, carry):
        labp[s, :, LANES : LANES + COLS] = labi[s].astype(F32).astype(BF16)
        return carry

    lax.fori_loop(0, SLICES, convert, 0)

    def alpha_copy(j):
        return remote(
            alpha_send.at[j],
            alpha_recv.at[me],
            alpha_ssem.at[j],
            alpha_rsem.at[me],
            (j, lat),
        )

    def alpha_arrival(j):
        return remote(
            alpha_send.at[j],
            alpha_recv.at[j],
            alpha_ssem.at[j],
            alpha_rsem.at[j],
            (j, lat),
        )

    def window(j):
        return pl.ds(pl.multiple_of(j * LANES, LANES), 3 * LANES)

    def opacities(j, carry):
        through = [jnp.ones((8, LANES), F32) for _ in range(4)]
        edge_tile = jnp.minimum(j, 1)
        for g in range(GROUPS):
            first = STEP * g
            values = volp[1 + first : 1 + first + STEP, :, window(j)]
            marks = labp[first : first + STEP, :, window(j)]
            both = jnp.concatenate([values, marks], axis=0)
            moved = dot(both.reshape(2 * STEP * ROWS, 3 * LANES), smat[g, :, 0:LANES])
            classes = moved[STEP * ROWS :].astype(jnp.int32)
            moved = moved[: STEP * ROWS]
            vs[j, g, 1 : 1 + STEP, BODY] = moved.reshape(STEP, ROWS, LANES)
            qs[j, first : first + STEP] = classes.reshape(STEP, ROWS, LANES)
            slopes = dot(values.reshape(STEP * ROWS, 3 * LANES), smat[g, :, LANES : 2 * LANES])
            gx[j, first : first + STEP] = slopes.reshape(STEP, ROWS, LANES)
            for i in range(STEP):
                factor = kvec[first + i, edge_tile]
                for rb in range(4):
                    at = i * ROWS + rb * 8
                    q = classes[at : at + 8]
                    x = lookup(tables[GAIN], q) * moved[at : at + 8]
                    x = x + lookup(tables[BIAS], q)
                    t = jnp.exp2(factor * jnp.log(1.0 + jnp.exp2(x)))
                    tc[j, first + i, rb * 8 : rb * 8 + 8] = t
                    through[rb] = through[rb] * t
        opaque = 1.0 - jnp.concatenate(through, axis=0)
        alpha_send[j] = opaque.reshape(2, HALF, LANES).astype(BF16)

        @pl.when(j != me)
        def _():
            alpha_copy(j).start()

        return carry

    lax.fori_loop(0, TILES, opacities, 0)
    alpha_recv[me] = alpha_send[me]

    def boundary(j):
        for g in range(GROUPS):
            lines = [volp[STEP * g, :, window(j)], volp[STEP * g + STEP + 1, :, window(j)]]
            lines += [rowp[0, :, window(j)], rowp[1, :, window(j)]]
            moved = dot(jnp.concatenate(lines, axis=0), smat[g, :, 0:LANES])
            below, above = moved[0:ROWS], moved[ROWS : 2 * ROWS]
            vs[j, g, 0, BODY] = below * not_first if g == 0 else below
            vs[j, g, STEP + 1, BODY] = above * not_last if g == GROUPS - 1 else above
            over = moved[2 * ROWS : 2 * ROWS + SLICES] * not_top
            under = moved[2 * ROWS + SLICES :] * not_bottom
            for i in range(STEP):
                s = STEP * g + i
                vs[j, g, 1 + i, 7:8] = over[s : s + 1]
                vs[j, g, 1 + i, 8 + ROWS : 9 + ROWS] = under[s : s + 1]

    def wait_alpha(i, carry):
        alpha_arrival(lax.rem(me + i, TILES)).wait_recv()
        return carry

    def distance_of(k):
        return jnp.where(lax.rem(k, 2) == 0, 4 - k // 2, k // 2 - 3)

    def front_copy(k):
        return remote(
            front_send.at[k],
            front_recv.at[me],
            front_ssem.at[k],
            front_rsem.at[me],
            (k, lat),
        )

    def front_arrival(k):
        return remote(
            front_send.at[k],
            front_recv.at[k],
            front_ssem.at[k],
            front_rsem.at[k],
            (k, lat),
        )

    def send_front(n, carry):
        other = lax.rem(chip - distance_of(n // 2) + CHIPS, CHIPS)
        k = 2 * other + jnp.where(lax.rem(n, 2) == 1, core, 1 - core)
        rank = jnp.int32(0)
        for j in range(TILES):
            rank = jnp.where(order[j] == k, j, rank)
        front_send[k] = jnp.round(front[rank] * UNIT).astype(jnp.int32).astype(jnp.int16)

        @pl.when(n < TILES - 1)
        def _():
            front_copy(k).start()

        return carry

    def exchange_fronts():
        lax.fori_loop(1, TILES, wait_alpha, 0)
        run = jnp.ones((2, HALF, LANES), F32)
        for j in range(TILES):
            front[j] = run
            run = run * (1.0 - alpha_recv[order[j]].astype(F32))
        opaque[...] = 1.0 - run
        lax.fori_loop(0, TILES, send_front, 0)
        front_recv[me] = front_send[me]

    def chunk_copy(k, p):
        return remote(
            chunk_send.at[k, p],
            chunk_recv.at[k, p],
            chunk_ssem.at[k, p],
            chunk_rsem.at[k, p],
            (jnp.where(lax.rem(k, 2) == 0, ahead, behind), lat),
        )

    def pair_copy(k):
        return remote(
            pair_send.at[k],
            pair_recv.at[k],
            pair_ssem.at[k],
            pair_rsem.at[k],
            (sibling, lat),
        )

    def render(tile, i_tile, h, rb):
        first = h * HALF + rb * 8
        r0 = pl.ds(pl.multiple_of(first, 8), 8)
        here = pl.ds(pl.multiple_of(first + 8, 8), 8)
        zero = jnp.zeros((8, LANES), F32)
        state = [zero] * SENT
        through = zero + 1.0
        for s in range(SLICES):
            g, i = s // STEP, s % STEP
            v = vs[tile, g, i + 1, here]
            below = vs[tile, g, i, here]
            above = vs[tile, g, i + 2, here]
            dx = gx[tile, s, r0]
            dy = vs[tile, g, i + 1, pl.ds(first + 9, 8)] - vs[tile, g, i + 1, pl.ds(first + 7, 8)]
            q = qs[tile, s, r0]
            dz = above - below
            inverse = lax.rsqrt(dx * dx + dy * dy + dz * dz + 4.0)
            later = through * tc[tile, s, r0]
            w = through - later
            through = later
            wn = w * inverse
            light = 0.288 * dx + 0.36 * dy + 0.384 * dz
            shaded = 0.4 * w + wn * jnp.maximum(light, 0.0)
            texture = 0.55 + 0.45 * jnp.tanh(below + above)
            plain = w * texture
            color = shaded * texture
            moving = w + (0.5 * w) * jnp.tanh(v)
            new = []
            tints = [lookup(tables[ALBEDO + c], q) for c in range(3)]
            new += [tint * color for tint in tints]
            new += [wn * dx, wn * dy, wn * dz]
            new += [tint * plain for tint in tints]
            new += [jnp.where(q == k, w, 0.0) for k in range(CLASSES - 1)]
            new += [lookup(tables[MOTION + c], q) * moving for c in range(2)]
            state = [a + b for a, b in zip(state, new)]
        final = state[0:16] + [a * (1.0 / MOTION_MAX) for a in state[16:18]]
        for c in range(SENT):
            part[i_tile, h, c, pl.ds(pl.multiple_of(rb * 8, 8), 8)] = final[c]

    def tile_of(i):
        kept = lax.rem(i, 2)
        tile_chip = lax.rem(chip + distance_of(i // 2) + CHIPS, CHIPS)
        return 2 * tile_chip + jnp.where(kept == 1, core, 1 - core)

    def scaled(i, p):
        h = p // (SENT // GROUP)
        channels = pl.ds(GROUP * lax.rem(p, SENT // GROUP), GROUP)
        image = part[i, h, channels].astype(BF16).astype(F32)
        return image * front_recv[tile_of(i), h].astype(jnp.int32).astype(F32)[None]

    def codes(i, p):
        return jnp.round(scaled(i, p)).astype(jnp.int32)

    def to_sibling(k):
        front_arrival(tile_of(2 * k)).wait_recv()

        def piece(p, carry):
            pair_send[k, p] = codes(2 * k, p).astype(jnp.int16)
            return carry

        lax.fori_loop(0, PIECES, piece, 0)
        pair_copy(k).start()

    def onward(k):
        pair_copy(k).wait_recv()
        front_arrival(tile_of(2 * k + 1)).wait_recv()

        def piece(p, carry):
            own = codes(2 * k + 1, p) + pair_recv[k, p].astype(jnp.int32)

            @pl.when(k < 2)
            def _():
                chunk_send[k, p] = own.astype(jnp.int16)

            @pl.when(k >= 2)
            def _():
                chunk_copy(k - 2, p).wait_recv()
                total = own + chunk_recv[k - 2, p].astype(jnp.int32)
                chunk_send[k, p] = total.astype(jnp.int16)

            chunk_copy(k, p).start()
            return carry

        lax.fori_loop(0, PIECES, piece, 0)

    def tile_step(i, carry):
        tile = tile_of(i)
        boundary(tile)

        def row_block(n, inner_carry):
            render(tile, i, n // 2, lax.rem(n, 2))
            return inner_carry

        lax.fori_loop(0, 4, row_block, 0)

        @pl.when(i == 1)
        def _():
            exchange_fronts()

        @pl.when(i == FRONT_AT)
        def _():
            def early_pair(k, inner_carry):
                to_sibling(k)
                return inner_carry

            lax.fori_loop(0, FRONT_AT // 2 + 1, early_pair, 0)

        @pl.when((i > FRONT_AT) & (lax.rem(i, 2) == 0))
        def _():
            to_sibling(i // 2)

        for at in sorted(set(ONWARD_AT.values())):

            @pl.when(i == at)
            def _(at=at):
                steps = [k for k in ONWARD_AT if ONWARD_AT[k] == at]

                def step(k, inner_carry):
                    onward(k)
                    return inner_carry

                lax.fori_loop(steps[0], steps[-1] + 1, step, 0)

        return carry

    for copy in halo:
        copy.wait()
    lax.fori_loop(0, TILES, tile_step, 0)

    turn = hot(iota((CHANNELS, CHANNELS), 0) == iota((CHANNELS, CHANNELS), 1)).astype(BF16)
    first_tmp[...] = jnp.zeros_like(first_tmp)
    second_tmp[...] = jnp.zeros_like(second_tmp)
    for dc in range(3):
        base = jnp.zeros((HIDDEN, 2 * LANES), F32)
        base2 = jnp.zeros((8, 3 * LANES), F32)
        for dr in range(3):
            first_tmp[:, 0:CHANNELS] = dot_first(conv_first[dr, dc], turn)
            wide = first_tmp[...]
            base = base + (pltpu.roll(wide, SLOTS * dr, 1) if dr else wide)
            second_tmp[0:3, 0:HIDDEN] = conv_second[dr, dc].astype(F32)
            wide = second_tmp[...]
            base2 = base2 + (pltpu.roll(wide, HIDDEN * dr, 1) if dr else wide)
        for i in range(8):
            moved = pltpu.roll(base, SLOTS * i, 1) if i else base
            first_mat[dc, i * HIDDEN : (i + 1) * HIDDEN, :] = moved.astype(BF16)
            moved = pltpu.roll(base2, HIDDEN * i, 1) if i else base2
            for c in range(3):
                second_mat[dc, c * 8 + i : c * 8 + i + 1, :] = moved[c : c + 1]

    n = iota((1, 6 * LANES), 1)
    tap = n // (2 * LANES) - 1
    spot = lax.rem(n, 2 * LANES)
    column = jnp.where(
        spot < LANES,
        spot + tap,
        jnp.where(
            spot == LANES, tap - 1, jnp.where(spot == LANES + 1, LANES + tap, -9)
        ),
    )
    own_shift[...] = hot(iota((LANES, 6 * LANES), 0) == column).astype(BF16)
    k16 = iota((16, 6 * LANES), 0)
    wanted = jnp.where(
        k16 < 2, k16 - 2, jnp.where((k16 == 10) | (k16 == 11), k16 + LANES - 10, -99)
    )
    rim_shift[...] = hot(wanted == column).astype(BF16)
    n = iota((1, 3 * LANES), 1)
    column = lax.rem(n, LANES) + n // LANES - 1
    source = jnp.where(column < 0, LANES, jnp.where(column == LANES, LANES + 1, column))
    second_shift[...] = hot(iota((2 * LANES, 3 * LANES), 0) == source).astype(BF16)
    x_first[:, OWN_END + OWN :, :] = jnp.zeros((3, FEATS - OWN_END - OWN, 2 * LANES), BF16)

    onward(jnp.int32(CHIPS - 2))

    def keep(c, row, block):
        aovs[c, row : row + 8] = block
        start = OWN + row * SLOTS + c
        feat[pl.ds(start, 8, stride=SLOTS), :] = block.astype(BF16).astype(F32)

    pair_copy(CHIPS - 1).wait_recv()
    for h in range(2):
        blocks = []
        for piece in range(PIECES // 2):
            p = h * (PIECES // 2) + piece
            chunk_copy(CHIPS - 3, p).wait_recv()
            chunk_copy(CHIPS - 2, p).wait_recv()
            summed = pair_recv[CHIPS - 1, p].astype(jnp.int32)
            summed = summed + chunk_recv[CHIPS - 3, p].astype(jnp.int32)
            summed = summed + chunk_recv[CHIPS - 2, p].astype(jnp.int32)
            total = scaled(TILES - 1, p) + summed.astype(F32)
            blocks += [total[c] for c in range(GROUP)]
        for rb in range(2):
            row = h * HALF + rb * 8
            lines = [block[rb * 8 : rb * 8 + 8] * (1.0 / UNIT) for block in blocks]
            opacity = opaque[h, rb * 8 : rb * 8 + 8]
            covered = lines[9:16]
            last = opacity - sum(covered[1:], covered[0])
            moved = [line * MOTION_MAX for line in lines[16:18]]
            final = lines[0:3] + [opacity] + lines[3:9] + covered + [last] + moved
            for c in range(CHANNELS):
                keep(c, row, final[c])

    pick = iota((8, LANES), 0)
    at = iota((8, LANES), 1)
    chosen = (
        ((pick == 0) & (at == LANES - 2))
        | ((pick == 1) & (at == LANES - 1))
        | ((pick == 2) & (at == 0))
        | ((pick == 3) & (at == 1))
    )
    rim = [
        remote(
            feat.at[pl.ds(OWN, OWN)],
            feat.at[pl.ds(OWN_END, OWN)],
            rim_ssem.at[0],
            rim_rsem.at[0],
            (me, up),
        ),
        remote(
            feat.at[pl.ds(OWN_END - OWN, OWN)],
            feat.at[pl.ds(0, OWN)],
            rim_ssem.at[1],
            rim_rsem.at[1],
            (me, down),
        ),
    ]
    rim[0].start()
    rim[1].start()
    edge[...] = dot_last(hot(chosen).astype(BF16), feat[OWN:OWN_END].astype(BF16))
    top = pl.ds(0, LANES)
    bottom = pl.ds(ROWS * SLOTS - LANES, LANES)
    targets = [
        (edge, edge_recv.at[0], (right, lat)),
        (edge, edge_recv.at[1], (left, lat)),
        (edge.at[:, top], corner_recv.at[0], (right, up)),
        (edge.at[:, top], corner_recv.at[1], (left, up)),
        (edge.at[:, bottom], corner_recv.at[2], (right, down)),
        (edge.at[:, bottom], corner_recv.at[3], (left, down)),
    ]
    for number, (src, dst, device) in enumerate(targets):
        copy = remote(src, dst, rim_ssem.at[2 + number], rim_rsem.at[2 + number], device)
        copy.start()
        rim.append(copy)

    def put(start, end, values, add):
        for dc in range(3):
            for side in range(2):
                if add and dc == 1 and side == 0:
                    continue
                at = 2 * dc + side
                block = values[:, at * LANES : (at + 1) * LANES].astype(BF16)
                lanes = slice(side * LANES, (side + 1) * LANES)
                if add:
                    block = block + x_first[dc, start:end, lanes]
                x_first[dc, start:end, lanes] = block

    put(OWN, OWN_END, dot(feat[OWN:OWN_END].astype(BF16), own_shift[...]), False)
    for copy in rim:
        copy.wait()

    def both(first, second):
        return jnp.concatenate([first * not_first, second * not_last], axis=0).astype(BF16)

    put(OWN, OWN_END, dot_first(both(edge_recv[0], edge_recv[1]), rim_shift[...]), True)
    lower = dot_first(both(corner_recv[0], corner_recv[1]), rim_shift[...])
    upper = dot_first(both(corner_recv[2], corner_recv[3]), rim_shift[...])
    over = dot(feat[0:OWN].astype(BF16), own_shift[...])
    under = dot(feat[OWN_END : OWN_END + OWN].astype(BF16), own_shift[...])
    put(0, OWN, (over + upper[LANES - OWN :]) * not_top, False)
    put(OWN_END, OWN_END + OWN, (under + lower[0:OWN]) * not_bottom, False)

    eye = iota((HIDDEN, HIDDEN), 0) == iota((HIDDEN, HIDDEN), 1)
    bias_col = jnp.sum(jnp.where(eye, bias_first[...], 0.0), axis=1, keepdims=True)
    bias_all = jnp.concatenate([bias_col] * 8, axis=0)
    spot = iota((1, 2 * LANES), 1)
    inside = jnp.where(
        spot == LANES, not_first, jnp.where(spot == LANES + 1, not_last, 1.0)
    )
    row_of = iota((8 * HIDDEN, 1), 0) // HIDDEN
    for b in range(5):
        total = jnp.zeros((8 * HIDDEN, 2 * LANES), F32)
        for dc in range(3):
            x = x_first[dc, 8 * SLOTS * b : 8 * SLOTS * b + 2 * LANES, :]
            total = total + dot(first_mat[dc], x)
        total = jnp.maximum(total + bias_all, 0.0) * inside
        if b == 0:
            total = total * jnp.where(row_of == 0, not_top, 1.0)
        if b == 4:
            total = total * jnp.where(row_of == 1, not_bottom, 1.0)
        hidden[8 * HIDDEN * b : 8 * HIDDEN * (b + 1), :] = total.astype(BF16)

    moved = dot(hidden[...], second_shift[...])
    for dc in range(3):
        x_second[dc] = moved[:, dc * LANES : (dc + 1) * LANES].astype(BF16)
    for b in range(4):
        total = jnp.zeros((3 * 8, LANES), F32)
        for dc in range(3):
            x = x_second[dc, 8 * HIDDEN * b : 8 * HIDDEN * b + 10 * HIDDEN, :]
            total = total + dot(second_mat[dc][:, 0 : 10 * HIDDEN].astype(BF16), x)
        for c in range(3):
            rows = slice(8 * b, 8 * b + 8)
            color = aovs[c, rows] + total[8 * c : 8 * c + 8]
            denoised[c, rows] = color + bias_second[c]

    def sent(k, carry):
        other = lax.rem(me + k, TILES)
        alpha_copy(other).wait_send()
        front_copy(other).wait_send()
        return carry

    def passed(k, carry):
        for p in range(PIECES):
            chunk_copy(k, p).wait_send()
        return carry

    def paired(k, carry):
        pair_copy(k).wait_send()
        return carry

    lax.fori_loop(1, TILES, sent, 0)
    lax.fori_loop(0, CHIPS - 1, passed, 0)
    lax.fori_loop(0, CHIPS, paired, 0)


def per_device(
    volume,
    labels,
    active_slices,
    view_order,
    density_gain,
    density_bias,
    albedo_table,
    motion_table,
    conv_first,
    bias_first,
    conv_second,
    bias_second,
):
    smem = pl.BlockSpec(memory_space=pltpu.SMEM)
    vmem = pl.BlockSpec(memory_space=pltpu.VMEM)
    anywhere = pl.BlockSpec(memory_space=pl.ANY)
    cells = (TILES, SLICES, ROWS, LANES)
    tile = (TILES, 2, HALF, LANES)
    chunk = (CHANNELS, ROWS, LANES)
    pieces = (PIECES, GROUP, HALF, LANES)
    dma = pltpu.SemaphoreType.DMA
    return pl.pallas_call(
        kernel,
        out_shape=(
            jax.ShapeDtypeStruct(chunk, F32),
            jax.ShapeDtypeStruct((3, ROWS, LANES), F32),
        ),
        in_specs=[anywhere, anywhere] + [smem] * 6 + [vmem] * 3 + [smem],
        out_specs=(vmem, vmem),
        scratch_shapes=[
            pltpu.VMEM((SLICES + 2, ROWS, WIDE), BF16),
            pltpu.VMEM((SLICES, ROWS, COLS), jnp.int32),
            pltpu.VMEM((SLICES, ROWS, WIDE), BF16),
            pltpu.VMEM((SLICES, COLS), F32),
            pltpu.VMEM((2, SLICES, COLS), BF16),
            pltpu.VMEM((2, SLICES, WIDE), BF16),
            pltpu.VMEM((GROUPS, 3 * LANES, 2 * LANES), BF16),
            pltpu.VMEM((SLICES, 2, 8, LANES), F32),
            pltpu.VMEM((7, CLASSES, LANES), F32),
            pltpu.VMEM((TILES, GROUPS, STEP + 2, ROWS + 16, LANES), F32),
            pltpu.VMEM(cells, F32),
            pltpu.VMEM(cells, F32),
            pltpu.VMEM(cells, jnp.int32),
            pltpu.VMEM(tile, BF16),
            pltpu.VMEM(tile, BF16),
            pltpu.VMEM(tile, F32),
            pltpu.VMEM(tile, jnp.int16),
            pltpu.VMEM(tile, jnp.int16),
            pltpu.VMEM((TILES, 2, SENT, HALF, LANES), F32),
            pltpu.VMEM((2, HALF, LANES), F32),
            pltpu.VMEM((CHIPS,) + pieces, jnp.int16),
            pltpu.VMEM((CHIPS,) + pieces, jnp.int16),
            pltpu.VMEM((CHIPS - 1,) + pieces, jnp.int16),
            pltpu.VMEM((CHIPS - 1,) + pieces, jnp.int16),
            pltpu.VMEM((FEATS, LANES), F32),
            pltpu.VMEM((8, ROWS * SLOTS), F32),
            pltpu.VMEM((2, 8, ROWS * SLOTS), F32),
            pltpu.VMEM((4, 8, LANES), F32),
            pltpu.VMEM((HIDDEN, 2 * LANES), F32),
            pltpu.VMEM((3, 8 * HIDDEN, 2 * LANES), BF16),
            pltpu.VMEM((8, 3 * LANES), F32),
            pltpu.VMEM((3, 24, 3 * LANES), F32),
            pltpu.VMEM((3, FEATS, 2 * LANES), BF16),
            pltpu.VMEM((40 * HIDDEN, 2 * LANES), BF16),
            pltpu.VMEM((3, 40 * HIDDEN, LANES), BF16),
            pltpu.VMEM((LANES, 6 * LANES), BF16),
            pltpu.VMEM((16, 6 * LANES), BF16),
            pltpu.VMEM((2 * LANES, 3 * LANES), BF16),
            dma((2,)),
            dma((4,)),
            dma((4,)),
            dma((TILES,)),
            dma((TILES,)),
            dma((TILES,)),
            dma((TILES,)),
            dma((CHIPS,)),
            dma((CHIPS,)),
            dma((CHIPS - 1, PIECES)),
            dma((CHIPS - 1, PIECES)),
            dma((8,)),
            dma((8,)),
        ],
        compiler_params=pltpu.CompilerParams(
            collective_id=0, has_side_effects=True, vmem_limit_bytes=60 * 1024 * 1024
        ),
    )(
        volume,
        labels,
        active_slices,
        view_order,
        density_gain,
        density_bias,
        albedo_table,
        motion_table,
        jnp.swapaxes(conv_first, 2, 3),
        bias_first.reshape(1, HIDDEN),
        conv_second,
        bias_second,
    )


def solution(mesh):
    placed = (P("depth", "lat", None),) * 2 + (P("depth", "lat"),) + (P(),) * 9
    return jax.shard_map(
        per_device,
        mesh=mesh,
        in_specs=placed,
        out_specs=(P(None, "lat", "depth"), P(None, "lat", "depth")),
        check_vma=False,
    )
```

```python
import jax
import jax.numpy as jnp
from jax import lax
from jax.experimental import pallas as pl
from jax.experimental.pallas import tpu as pltpu
from jax.sharding import PartitionSpec as P

MESH = pl.DeviceIdType.MESH
F32, BF16 = jnp.float32, jnp.bfloat16

SLICES = 16
ROWS = 32
COLS = 2048
LANES = 128
TILES = 16
BANDS = 16
CLASSES = 8
CHANNELS = 20
SLOTS = 24
HIDDEN = 32
GROUPS = 4
STEP = 4
WIDE = COLS + 2 * LANES
OPTICAL = 2.0 / 256
LOG2E = 1.4426950408889634
UNIT = 32000.0
MOTION_MAX = 8.0
CHIPS = TILES // 2
SENT = 18
GROUP = 18
PIECES = 2 * SENT // GROUP
FRONT_AT = 4
ONWARD_AT = {
    4: ((0, 0), (0, 1)),
    5: ((1, 0), (1, 1)),
    8: ((2, 0),),
    9: ((2, 1),),
    10: ((3, 0), (3, 1)),
    12: ((4, 0),),
    13: ((4, 1),),
    14: ((5, 0), (5, 1)),
}
HALF = 16
BODY = slice(8, 8 + ROWS)
OWN = 2 * SLOTS
OWN_END = OWN + ROWS * SLOTS
FEATS = 1024
GAIN, BIAS, ALBEDO, MOTION = 0, 1, 2, 5


def dot(a, b):
    return jnp.dot(a, b, preferred_element_type=F32)


def dot_first(a, b):
    return lax.dot_general(a, b, (((0,), (0,)), ((), ())), preferred_element_type=F32)


def dot_last(a, b):
    return lax.dot_general(a, b, (((1,), (1,)), ((), ())), preferred_element_type=F32)


def iota(shape, dim):
    return lax.broadcasted_iota(jnp.int32, shape, dim)


def hot(mask):
    return jnp.where(mask, 1.0, 0.0).astype(F32)


def lookup(table, index):
    return jnp.take_along_axis(table, index, axis=0, mode="promise_in_bounds")


def kernel(
    vol,
    lab,
    active,
    order,
    gain,
    bias,
    albedo,
    motion,
    conv_first,
    bias_first,
    conv_second,
    bias_second,
    aovs,
    denoised,
    volp,
    labi,
    labp,
    row_tmp,
    row_send,
    rowp,
    smat,
    kvec,
    tables,
    vs,
    gx,
    tc,
    qs,
    alpha_send,
    alpha_recv,
    front,
    front_send,
    front_recv,
    part,
    opaque,
    pair_send,
    pair_recv,
    chunk_send,
    chunk_recv,
    feat,
    edge,
    edge_recv,
    corner_recv,
    first_tmp,
    first_mat,
    second_tmp,
    second_mat,
    x_first,
    hidden,
    x_second,
    own_shift,
    rim_shift,
    second_shift,
    load_sem,
    halo_ssem,
    halo_rsem,
    alpha_ssem,
    alpha_rsem,
    front_ssem,
    front_rsem,
    pair_ssem,
    pair_rsem,
    chunk_ssem,
    chunk_rsem,
    rim_ssem,
    rim_rsem,
):
    me = lax.axis_index("depth")
    lat = lax.axis_index("lat")
    core = lax.rem(me, 2)
    chip = me // 2
    sibling = me + 1 - 2 * core
    ahead = lax.rem(me + 2, TILES)
    behind = lax.rem(me + TILES - 2, TILES)
    right = lax.rem(me + 1, TILES)
    left = lax.rem(me + TILES - 1, TILES)
    down = lax.rem(lat + 1, BANDS)
    up = lax.rem(lat + BANDS - 1, BANDS)
    not_first = hot(me > 0)
    not_last = hot(me < TILES - 1)
    not_top = hot(lat > 0)
    not_bottom = hot(lat < BANDS - 1)

    def remote(src, dst, ssem, rsem, device):
        return pltpu.make_async_remote_copy(
            src_ref=src,
            dst_ref=dst,
            send_sem=ssem,
            recv_sem=rsem,
            device_id=device,
            device_id_type=MESH,
        )

    load_vol = pltpu.make_async_copy(
        vol, volp.at[pl.ds(1, SLICES), :, pl.ds(LANES, COLS)], load_sem.at[0]
    )
    load_lab = pltpu.make_async_copy(lab, labi, load_sem.at[1])
    load_vol.start()
    load_lab.start()

    barrier = pltpu.get_barrier_semaphore()

    def greet(device):
        pl.semaphore_signal(barrier, inc=1, device_id=device, device_id_type=MESH)

    def greet_peer(i, carry):
        greet((lax.rem(me + i, TILES), lat))
        return carry

    lax.fori_loop(1, TILES, greet_peer, 0)
    for row in (up, down):
        for col in (left, me, right):
            greet((col, row))

    side = jnp.zeros((SLICES + 2, ROWS, LANES), BF16)
    volp[:, :, 0:LANES] = side
    volp[:, :, LANES + COLS :] = side
    labp[:, :, 0:LANES] = side[:SLICES]
    labp[:, :, LANES + COLS :] = side[:SLICES]
    rowp[:, :, 0:LANES] = side[0:2, 0:SLICES]
    rowp[:, :, LANES + COLS :] = side[0:2, 0:SLICES]
    feat[OWN:OWN_END] = jnp.zeros((ROWS * SLOTS, LANES), F32)

    class_of = iota((CLASSES, LANES), 0)
    sources = (
        [(gain, None), (bias, None)]
        + [(albedo, c) for c in range(3)]
        + [(motion, c) for c in range(2)]
    )
    for number, (ref, row) in enumerate(sources):
        table = jnp.zeros((CLASSES, LANES), F32)
        for k in range(CLASSES):
            value = ref[k] if row is None else ref[row, k]
            table = jnp.where(class_of == k, value, table)
        tables[number] = table * LOG2E if number < ALBEDO else table
    source_col = iota((3 * LANES, 2 * LANES), 0) - LANES
    target = iota((3 * LANES, 2 * LANES), 1)
    lane = lax.rem(target, LANES)
    for g in range(GROUPS):
        delta = source_col - lane + (STEP * me + g)
        smat[g] = jnp.where(
            target < LANES, hot(delta == 0), hot(delta == 1) - hot(delta == -1)
        ).astype(BF16)
    lane8 = iota((8, LANES), 1)
    for s in range(SLICES):
        factor = jnp.where(s < active[0, 0], -OPTICAL * LOG2E, 0.0).astype(F32)
        kvec[s, 1] = jnp.zeros((8, LANES), F32) + factor
        kvec[s, 0] = jnp.where(lane8 >= STEP * me + s // STEP, factor, 0.0)

    load_vol.wait()
    pl.semaphore_wait(barrier, TILES - 1 + 6)

    inner = pl.ds(LANES, COLS)
    halo = [
        remote(
            volp.at[SLICES, :, inner],
            volp.at[0, :, inner],
            halo_ssem.at[0],
            halo_rsem.at[0],
            (right, lat),
        ),
        remote(
            volp.at[1, :, inner],
            volp.at[SLICES + 1, :, inner],
            halo_ssem.at[1],
            halo_rsem.at[1],
            (left, lat),
        ),
        remote(
            row_send.at[1],
            rowp.at[0, :, inner],
            halo_ssem.at[2],
            halo_rsem.at[2],
            (me, down),
        ),
        remote(
            row_send.at[0],
            rowp.at[1, :, inner],
            halo_ssem.at[3],
            halo_rsem.at[3],
            (me, up),
        ),
    ]
    halo[0].start()
    halo[1].start()
    for end in range(2):
        for s in range(SLICES):
            rows = volp[s + 1, 16 * end : 16 * end + 16, LANES : LANES + COLS].astype(F32)
            row_tmp[s : s + 1, :] = rows[15:16] if end else rows[0:1]
        row_send[end] = row_tmp[...].astype(BF16)
    halo[2].start()
    halo[3].start()

    load_lab.wait()

    def convert(s, carry):
        labp[s, :, LANES : LANES + COLS] = labi[s].astype(F32).astype(BF16)
        return carry

    lax.fori_loop(0, SLICES, convert, 0)

    def alpha_copy(j):
        return remote(
            alpha_send.at[j],
            alpha_recv.at[me],
            alpha_ssem.at[j],
            alpha_rsem.at[me],
            (j, lat),
        )

    def alpha_arrival(j):
        return remote(
            alpha_send.at[j],
            alpha_recv.at[j],
            alpha_ssem.at[j],
            alpha_rsem.at[j],
            (j, lat),
        )

    def window(j):
        return pl.ds(pl.multiple_of(j * LANES, LANES), 3 * LANES)

    def opacities(j, carry):
        through = [jnp.ones((8, LANES), F32) for _ in range(4)]
        edge_tile = jnp.minimum(j, 1)
        for g in range(GROUPS):
            first = STEP * g
            values = volp[1 + first : 1 + first + STEP, :, window(j)]
            marks = labp[first : first + STEP, :, window(j)]
            both = jnp.concatenate([values, marks], axis=0)
            moved = dot(both.reshape(2 * STEP * ROWS, 3 * LANES), smat[g, :, 0:LANES])
            classes = moved[STEP * ROWS :].astype(jnp.int32)
            moved = moved[: STEP * ROWS]
            vs[j, g, 1 : 1 + STEP, BODY] = moved.reshape(STEP, ROWS, LANES)
            qs[j, first : first + STEP] = classes.reshape(STEP, ROWS, LANES)
            slopes = dot(values.reshape(STEP * ROWS, 3 * LANES), smat[g, :, LANES : 2 * LANES])
            gx[j, first : first + STEP] = slopes.reshape(STEP, ROWS, LANES)
            for i in range(STEP):
                factor = kvec[first + i, edge_tile]
                for rb in range(4):
                    at = i * ROWS + rb * 8
                    q = classes[at : at + 8]
                    x = lookup(tables[GAIN], q) * moved[at : at + 8]
                    x = x + lookup(tables[BIAS], q)
                    t = jnp.exp2(factor * jnp.log(1.0 + jnp.exp2(x)))
                    tc[j, first + i, rb * 8 : rb * 8 + 8] = t
                    through[rb] = through[rb] * t
        opaque = 1.0 - jnp.concatenate(through, axis=0)
        alpha_send[j] = opaque.reshape(2, HALF, LANES).astype(BF16)

        @pl.when(j != me)
        def _():
            alpha_copy(j).start()

        return carry

    lax.fori_loop(0, TILES, opacities, 0)
    alpha_recv[me] = alpha_send[me]

    def boundary(first_tile):
        for g in range(GROUPS):
            lines = []
            for j in (first_tile, first_tile + 1):
                lines += [volp[STEP * g, :, window(j)], volp[STEP * g + STEP + 1, :, window(j)]]
                lines += [rowp[0, :, window(j)], rowp[1, :, window(j)]]
            both_tiles = dot(jnp.concatenate(lines, axis=0), smat[g, :, 0:LANES])
            for number in range(2):
                j = first_tile + number
                moved = both_tiles[number * 3 * ROWS : (number + 1) * 3 * ROWS]
                below, above = moved[0:ROWS], moved[ROWS : 2 * ROWS]
                vs[j, g, 0, BODY] = below * not_first if g == 0 else below
                vs[j, g, STEP + 1, BODY] = above * not_last if g == GROUPS - 1 else above
                over = moved[2 * ROWS : 2 * ROWS + SLICES] * not_top
                under = moved[2 * ROWS + SLICES :] * not_bottom
                for i in range(STEP):
                    s = STEP * g + i
                    vs[j, g, 1 + i, 7:8] = over[s : s + 1]
                    vs[j, g, 1 + i, 8 + ROWS : 9 + ROWS] = under[s : s + 1]

    def wait_alpha(i, carry):
        alpha_arrival(lax.rem(me + i, TILES)).wait_recv()
        return carry

    def distance_of(k):
        return jnp.where(lax.rem(k, 2) == 0, 4 - k // 2, k // 2 - 3)

    def front_copy(k):
        return remote(
            front_send.at[k],
            front_recv.at[me],
            front_ssem.at[k],
            front_rsem.at[me],
            (k, lat),
        )

    def front_arrival(k):
        return remote(
            front_send.at[k],
            front_recv.at[k],
            front_ssem.at[k],
            front_rsem.at[k],
            (k, lat),
        )

    def send_front(n, carry):
        other = lax.rem(chip - distance_of(n // 2) + CHIPS, CHIPS)
        k = 2 * other + jnp.where(lax.rem(n, 2) == 1, core, 1 - core)
        rank = jnp.int32(0)
        for j in range(TILES):
            rank = jnp.where(order[j] == k, j, rank)
        front_send[k] = jnp.round(front[rank] * UNIT).astype(jnp.int32).astype(jnp.int16)

        @pl.when(n < TILES - 1)
        def _():
            front_copy(k).start()

        return carry

    def exchange_fronts():
        lax.fori_loop(1, TILES, wait_alpha, 0)
        run = jnp.ones((2, HALF, LANES), F32)
        for j in range(TILES):
            front[j] = run
            run = run * (1.0 - alpha_recv[order[j]].astype(F32))
        opaque[...] = 1.0 - run
        lax.fori_loop(0, TILES, send_front, 0)
        front_recv[me] = front_send[me]

    def chunk_copy(k, p):
        return remote(
            chunk_send.at[k, p],
            chunk_recv.at[k, p],
            chunk_ssem.at[k, p],
            chunk_rsem.at[k, p],
            (jnp.where(lax.rem(k, 2) == 0, ahead, behind), lat),
        )

    def pair_copy(k):
        return remote(
            pair_send.at[k],
            pair_recv.at[k],
            pair_ssem.at[k],
            pair_rsem.at[k],
            (sibling, lat),
        )

    def render(tile, i_tile, h, rb):
        first = h * HALF + rb * 8
        r0 = pl.ds(pl.multiple_of(first, 8), 8)
        here = pl.ds(pl.multiple_of(first + 8, 8), 8)
        zero = jnp.zeros((8, LANES), F32)
        state = [zero] * SENT
        through = zero + 1.0
        for s in range(SLICES):
            g, i = s // STEP, s % STEP
            v = vs[tile, g, i + 1, here]
            below = vs[tile, g, i, here]
            above = vs[tile, g, i + 2, here]
            dx = gx[tile, s, r0]
            dy = vs[tile, g, i + 1, pl.ds(first + 9, 8)] - vs[tile, g, i + 1, pl.ds(first + 7, 8)]
            q = qs[tile, s, r0]
            dz = above - below
            inverse = lax.rsqrt(dx * dx + dy * dy + dz * dz + 4.0)
            later = through * tc[tile, s, r0]
            w = through - later
            through = later
            wn = w * inverse
            light = 0.288 * dx + 0.36 * dy + 0.384 * dz
            shaded = 0.4 * w + wn * jnp.maximum(light, 0.0)
            texture = 0.55 + 0.45 * jnp.tanh(below + above)
            plain = w * texture
            color = shaded * texture
            moving = w + (0.5 * w) * jnp.tanh(v)
            new = []
            tints = [lookup(tables[ALBEDO + c], q) for c in range(3)]
            new += [tint * color for tint in tints]
            new += [wn * dx, wn * dy, wn * dz]
            new += [tint * plain for tint in tints]
            new += [jnp.where(q == k, w, 0.0) for k in range(CLASSES - 1)]
            new += [lookup(tables[MOTION + c], q) * moving for c in range(2)]
            state = [a + b for a, b in zip(state, new)]
        final = state[0:16] + [a * (1.0 / MOTION_MAX) for a in state[16:18]]
        for c in range(SENT):
            part[i_tile, h, c, pl.ds(pl.multiple_of(rb * 8, 8), 8)] = final[c]

    def tile_of(i):
        kept = lax.rem(i, 2)
        tile_chip = lax.rem(chip + distance_of(i // 2) + CHIPS, CHIPS)
        return 2 * tile_chip + jnp.where(kept == 1, core, 1 - core)

    def scaled(i, p):
        h = p // (SENT // GROUP)
        channels = pl.ds(GROUP * lax.rem(p, SENT // GROUP), GROUP)
        image = part[i, h, channels].astype(BF16).astype(F32)
        return image * front_recv[tile_of(i), h].astype(jnp.int32).astype(F32)[None]

    def codes(i, p):
        return jnp.round(scaled(i, p)).astype(jnp.int32)

    def to_sibling(k):
        front_arrival(tile_of(2 * k)).wait_recv()

        def piece(p, carry):
            pair_send[k, p] = codes(2 * k, p).astype(jnp.int16)
            return carry

        lax.fori_loop(0, PIECES, piece, 0)
        pair_copy(k).start()

    def onward(k, p):
        if p == 0:
            pair_copy(k).wait_recv()
            front_arrival(tile_of(2 * k + 1)).wait_recv()
        total = codes(2 * k + 1, p) + pair_recv[k, p].astype(jnp.int32)
        if k >= 2:
            chunk_copy(k - 2, p).wait_recv()
            total = total + chunk_recv[k - 2, p].astype(jnp.int32)
        chunk_send[k, p] = total.astype(jnp.int16)
        chunk_copy(k, p).start()

    def tile_step(i, carry):
        tile = tile_of(i)

        @pl.when(lax.rem(i, 2) == 0)
        def _():
            boundary(2 * (tile // 2))


        def row_block(n, inner_carry):
            render(tile, i, n // 2, lax.rem(n, 2))
            return inner_carry

        lax.fori_loop(0, 4, row_block, 0)

        @pl.when(i == 1)
        def _():
            exchange_fronts()

        @pl.when(i == FRONT_AT)
        def _():
            def early_pair(k, inner_carry):
                to_sibling(k)
                return inner_carry

            lax.fori_loop(0, FRONT_AT // 2 + 1, early_pair, 0)

        @pl.when((i > FRONT_AT) & (lax.rem(i, 2) == 0))
        def _():
            to_sibling(i // 2)

        for at, pieces in ONWARD_AT.items():

            @pl.when(i == at)
            def _(pieces=pieces):
                for k, p in pieces:
                    onward(k, p)

        return carry

    for copy in halo:
        copy.wait()
    lax.fori_loop(0, TILES, tile_step, 0)

    turn = hot(iota((CHANNELS, CHANNELS), 0) == iota((CHANNELS, CHANNELS), 1)).astype(BF16)
    first_tmp[...] = jnp.zeros_like(first_tmp)
    second_tmp[...] = jnp.zeros_like(second_tmp)
    for dc in range(3):
        base = jnp.zeros((HIDDEN, 2 * LANES), F32)
        base2 = jnp.zeros((8, 3 * LANES), F32)
        for dr in range(3):
            first_tmp[:, 0:CHANNELS] = dot_first(conv_first[dr, dc], turn)
            wide = first_tmp[...]
            base = base + (pltpu.roll(wide, SLOTS * dr, 1) if dr else wide)
            second_tmp[0:3, 0:HIDDEN] = conv_second[dr, dc].astype(F32)
            wide = second_tmp[...]
            base2 = base2 + (pltpu.roll(wide, HIDDEN * dr, 1) if dr else wide)
        for i in range(8):
            moved = pltpu.roll(base, SLOTS * i, 1) if i else base
            first_mat[dc, i * HIDDEN : (i + 1) * HIDDEN, :] = moved.astype(BF16)
            moved = pltpu.roll(base2, HIDDEN * i, 1) if i else base2
            for c in range(3):
                second_mat[dc, c * 8 + i : c * 8 + i + 1, :] = moved[c : c + 1]

    n = iota((1, 6 * LANES), 1)
    tap = n // (2 * LANES) - 1
    spot = lax.rem(n, 2 * LANES)
    column = jnp.where(
        spot < LANES,
        spot + tap,
        jnp.where(
            spot == LANES, tap - 1, jnp.where(spot == LANES + 1, LANES + tap, -9)
        ),
    )
    own_shift[...] = hot(iota((LANES, 6 * LANES), 0) == column).astype(BF16)
    k16 = iota((16, 6 * LANES), 0)
    wanted = jnp.where(
        k16 < 2, k16 - 2, jnp.where((k16 == 10) | (k16 == 11), k16 + LANES - 10, -99)
    )
    rim_shift[...] = hot(wanted == column).astype(BF16)
    n = iota((1, 3 * LANES), 1)
    column = lax.rem(n, LANES) + n // LANES - 1
    source = jnp.where(column < 0, LANES, jnp.where(column == LANES, LANES + 1, column))
    second_shift[...] = hot(iota((2 * LANES, 3 * LANES), 0) == source).astype(BF16)
    x_first[:, OWN_END + OWN :, :] = jnp.zeros((3, FEATS - OWN_END - OWN, 2 * LANES), BF16)

    onward(CHIPS - 2, 0)
    onward(CHIPS - 2, 1)

    def keep(c, row, block):
        aovs[c, row : row + 8] = block
        start = OWN + row * SLOTS + c
        feat[pl.ds(start, 8, stride=SLOTS), :] = block.astype(BF16).astype(F32)

    pair_copy(CHIPS - 1).wait_recv()
    for h in range(2):
        blocks = []
        for piece in range(PIECES // 2):
            p = h * (PIECES // 2) + piece
            chunk_copy(CHIPS - 3, p).wait_recv()
            chunk_copy(CHIPS - 2, p).wait_recv()
            summed = pair_recv[CHIPS - 1, p].astype(jnp.int32)
            summed = summed + chunk_recv[CHIPS - 3, p].astype(jnp.int32)
            summed = summed + chunk_recv[CHIPS - 2, p].astype(jnp.int32)
            total = scaled(TILES - 1, p) + summed.astype(F32)
            blocks += [total[c] for c in range(GROUP)]
        for rb in range(2):
            row = h * HALF + rb * 8
            lines = [block[rb * 8 : rb * 8 + 8] * (1.0 / UNIT) for block in blocks]
            opacity = opaque[h, rb * 8 : rb * 8 + 8]
            covered = lines[9:16]
            last = opacity - sum(covered[1:], covered[0])
            moved = [line * MOTION_MAX for line in lines[16:18]]
            final = lines[0:3] + [opacity] + lines[3:9] + covered + [last] + moved
            for c in range(CHANNELS):
                keep(c, row, final[c])

    pick = iota((8, LANES), 0)
    at = iota((8, LANES), 1)
    chosen = (
        ((pick == 0) & (at == LANES - 2))
        | ((pick == 1) & (at == LANES - 1))
        | ((pick == 2) & (at == 0))
        | ((pick == 3) & (at == 1))
    )
    rim = [
        remote(
            feat.at[pl.ds(OWN, OWN)],
            feat.at[pl.ds(OWN_END, OWN)],
            rim_ssem.at[0],
            rim_rsem.at[0],
            (me, up),
        ),
        remote(
            feat.at[pl.ds(OWN_END - OWN, OWN)],
            feat.at[pl.ds(0, OWN)],
            rim_ssem.at[1],
            rim_rsem.at[1],
            (me, down),
        ),
    ]
    rim[0].start()
    rim[1].start()
    edge[...] = dot_last(hot(chosen).astype(BF16), feat[OWN:OWN_END].astype(BF16))
    top = pl.ds(0, LANES)
    bottom = pl.ds(ROWS * SLOTS - LANES, LANES)
    targets = [
        (edge, edge_recv.at[0], (right, lat)),
        (edge, edge_recv.at[1], (left, lat)),
        (edge.at[:, top], corner_recv.at[0], (right, up)),
        (edge.at[:, top], corner_recv.at[1], (left, up)),
        (edge.at[:, bottom], corner_recv.at[2], (right, down)),
        (edge.at[:, bottom], corner_recv.at[3], (left, down)),
    ]
    for number, (src, dst, device) in enumerate(targets):
        copy = remote(src, dst, rim_ssem.at[2 + number], rim_rsem.at[2 + number], device)
        copy.start()
        rim.append(copy)

    def put(start, end, values, add):
        for dc in range(3):
            for side in range(2):
                if add and dc == 1 and side == 0:
                    continue
                at = 2 * dc + side
                block = values[:, at * LANES : (at + 1) * LANES].astype(BF16)
                lanes = slice(side * LANES, (side + 1) * LANES)
                if add:
                    block = block + x_first[dc, start:end, lanes]
                x_first[dc, start:end, lanes] = block

    put(OWN, OWN_END, dot(feat[OWN:OWN_END].astype(BF16), own_shift[...]), False)
    for copy in rim:
        copy.wait()

    def both(first, second):
        return jnp.concatenate([first * not_first, second * not_last], axis=0).astype(BF16)

    put(OWN, OWN_END, dot_first(both(edge_recv[0], edge_recv[1]), rim_shift[...]), True)
    lower = dot_first(both(corner_recv[0], corner_recv[1]), rim_shift[...])
    upper = dot_first(both(corner_recv[2], corner_recv[3]), rim_shift[...])
    over = dot(feat[0:OWN].astype(BF16), own_shift[...])
    under = dot(feat[OWN_END : OWN_END + OWN].astype(BF16), own_shift[...])
    put(0, OWN, (over + upper[LANES - OWN :]) * not_top, False)
    put(OWN_END, OWN_END + OWN, (under + lower[0:OWN]) * not_bottom, False)

    eye = iota((HIDDEN, HIDDEN), 0) == iota((HIDDEN, HIDDEN), 1)
    bias_col = jnp.sum(jnp.where(eye, bias_first[...], 0.0), axis=1, keepdims=True)
    bias_all = jnp.concatenate([bias_col] * 8, axis=0)
    spot = iota((1, 2 * LANES), 1)
    inside = jnp.where(
        spot == LANES, not_first, jnp.where(spot == LANES + 1, not_last, 1.0)
    )
    row_of = iota((8 * HIDDEN, 1), 0) // HIDDEN
    for b in range(5):
        total = jnp.zeros((8 * HIDDEN, 2 * LANES), F32)
        for dc in range(3):
            x = x_first[dc, 8 * SLOTS * b : 8 * SLOTS * b + 2 * LANES, :]
            total = total + dot(first_mat[dc], x)
        total = jnp.maximum(total + bias_all, 0.0) * inside
        if b == 0:
            total = total * jnp.where(row_of == 0, not_top, 1.0)
        if b == 4:
            total = total * jnp.where(row_of == 1, not_bottom, 1.0)
        hidden[8 * HIDDEN * b : 8 * HIDDEN * (b + 1), :] = total.astype(BF16)

    moved = dot(hidden[...], second_shift[...])
    for dc in range(3):
        x_second[dc] = moved[:, dc * LANES : (dc + 1) * LANES].astype(BF16)
    for b in range(4):
        total = jnp.zeros((3 * 8, LANES), F32)
        for dc in range(3):
            x = x_second[dc, 8 * HIDDEN * b : 8 * HIDDEN * b + 10 * HIDDEN, :]
            total = total + dot(second_mat[dc][:, 0 : 10 * HIDDEN].astype(BF16), x)
        for c in range(3):
            rows = slice(8 * b, 8 * b + 8)
            color = aovs[c, rows] + total[8 * c : 8 * c + 8]
            denoised[c, rows] = color + bias_second[c]

    def sent(k, carry):
        other = lax.rem(me + k, TILES)
        alpha_copy(other).wait_send()
        front_copy(other).wait_send()
        return carry

    def passed(k, carry):
        for p in range(PIECES):
            chunk_copy(k, p).wait_send()
        return carry

    def paired(k, carry):
        pair_copy(k).wait_send()
        return carry

    lax.fori_loop(1, TILES, sent, 0)
    lax.fori_loop(0, CHIPS - 1, passed, 0)
    lax.fori_loop(0, CHIPS, paired, 0)


def per_device(
    volume,
    labels,
    active_slices,
    view_order,
    density_gain,
    density_bias,
    albedo_table,
    motion_table,
    conv_first,
    bias_first,
    conv_second,
    bias_second,
):
    smem = pl.BlockSpec(memory_space=pltpu.SMEM)
    vmem = pl.BlockSpec(memory_space=pltpu.VMEM)
    anywhere = pl.BlockSpec(memory_space=pl.ANY)
    cells = (TILES, SLICES, ROWS, LANES)
    tile = (TILES, 2, HALF, LANES)
    chunk = (CHANNELS, ROWS, LANES)
    pieces = (PIECES, GROUP, HALF, LANES)
    dma = pltpu.SemaphoreType.DMA
    return pl.pallas_call(
        kernel,
        out_shape=(
            jax.ShapeDtypeStruct(chunk, F32),
            jax.ShapeDtypeStruct((3, ROWS, LANES), F32),
        ),
        in_specs=[anywhere, anywhere] + [smem] * 6 + [vmem] * 3 + [smem],
        out_specs=(vmem, vmem),
        scratch_shapes=[
            pltpu.VMEM((SLICES + 2, ROWS, WIDE), BF16),
            pltpu.VMEM((SLICES, ROWS, COLS), jnp.int32),
            pltpu.VMEM((SLICES, ROWS, WIDE), BF16),
            pltpu.VMEM((SLICES, COLS), F32),
            pltpu.VMEM((2, SLICES, COLS), BF16),
            pltpu.VMEM((2, SLICES, WIDE), BF16),
            pltpu.VMEM((GROUPS, 3 * LANES, 2 * LANES), BF16),
            pltpu.VMEM((SLICES, 2, 8, LANES), F32),
            pltpu.VMEM((7, CLASSES, LANES), F32),
            pltpu.VMEM((TILES, GROUPS, STEP + 2, ROWS + 16, LANES), F32),
            pltpu.VMEM(cells, F32),
            pltpu.VMEM(cells, F32),
            pltpu.VMEM(cells, jnp.int32),
            pltpu.VMEM(tile, BF16),
            pltpu.VMEM(tile, BF16),
            pltpu.VMEM(tile, F32),
            pltpu.VMEM(tile, jnp.int16),
            pltpu.VMEM(tile, jnp.int16),
            pltpu.VMEM((TILES, 2, SENT, HALF, LANES), F32),
            pltpu.VMEM((2, HALF, LANES), F32),
            pltpu.VMEM((CHIPS,) + pieces, jnp.int16),
            pltpu.VMEM((CHIPS,) + pieces, jnp.int16),
            pltpu.VMEM((CHIPS - 1,) + pieces, jnp.int16),
            pltpu.VMEM((CHIPS - 1,) + pieces, jnp.int16),
            pltpu.VMEM((FEATS, LANES), F32),
            pltpu.VMEM((8, ROWS * SLOTS), F32),
            pltpu.VMEM((2, 8, ROWS * SLOTS), F32),
            pltpu.VMEM((4, 8, LANES), F32),
            pltpu.VMEM((HIDDEN, 2 * LANES), F32),
            pltpu.VMEM((3, 8 * HIDDEN, 2 * LANES), BF16),
            pltpu.VMEM((8, 3 * LANES), F32),
            pltpu.VMEM((3, 24, 3 * LANES), F32),
            pltpu.VMEM((3, FEATS, 2 * LANES), BF16),
            pltpu.VMEM((40 * HIDDEN, 2 * LANES), BF16),
            pltpu.VMEM((3, 40 * HIDDEN, LANES), BF16),
            pltpu.VMEM((LANES, 6 * LANES), BF16),
            pltpu.VMEM((16, 6 * LANES), BF16),
            pltpu.VMEM((2 * LANES, 3 * LANES), BF16),
            dma((2,)),
            dma((4,)),
            dma((4,)),
            dma((TILES,)),
            dma((TILES,)),
            dma((TILES,)),
            dma((TILES,)),
            dma((CHIPS,)),
            dma((CHIPS,)),
            dma((CHIPS - 1, PIECES)),
            dma((CHIPS - 1, PIECES)),
            dma((8,)),
            dma((8,)),
        ],
        compiler_params=pltpu.CompilerParams(
            collective_id=0, has_side_effects=True, vmem_limit_bytes=60 * 1024 * 1024
        ),
    )(
        volume,
        labels,
        active_slices,
        view_order,
        density_gain,
        density_bias,
        albedo_table,
        motion_table,
        jnp.swapaxes(conv_first, 2, 3),
        bias_first.reshape(1, HIDDEN),
        conv_second,
        bias_second,
    )


def solution(mesh):
    placed = (P("depth", "lat", None),) * 2 + (P("depth", "lat"),) + (P(),) * 9
    return jax.shard_map(
        per_device,
        mesh=mesh,
        in_specs=placed,
        out_specs=(P(None, "lat", "depth"), P(None, "lat", "depth")),
        check_vma=False,
    )
```

```python
import jax
import jax.numpy as jnp
from jax import lax
from jax.experimental import pallas as pl
from jax.experimental.pallas import tpu as pltpu
from jax.sharding import PartitionSpec as P

MESH = pl.DeviceIdType.MESH
F32, BF16 = jnp.float32, jnp.bfloat16

SLICES = 16
ROWS = 32
COLS = 2048
LANES = 128
TILES = 16
BANDS = 16
CLASSES = 8
CHANNELS = 20
SLOTS = 24
HIDDEN = 32
GROUPS = 4
STEP = 4
WIDE = COLS + 2 * LANES
OPTICAL = 2.0 / 256
LOG2E = 1.4426950408889634
UNIT = 32000.0
MOTION_MAX = 8.0
CHIPS = TILES // 2
SENT = 18
GROUP = 18
PIECES = 2 * SENT // GROUP
FRONT_AT = 4
ONWARD_AT = {4: ((0, 0), (0, 1)), 5: ((1, 0), (1, 1)), 8: ((2, 0),), 9: ((2, 1),), 10: ((3, 0), (3, 1)), 12: ((4, 0),), 13: ((4, 1),), 14: ((5, 0), (5, 1))}
HALF = 16
BODY = slice(8, 8 + ROWS)
OWN = 2 * SLOTS
OWN_END = OWN + ROWS * SLOTS
FEATS = 1024
GAIN, BIAS, ALBEDO, MOTION = 0, 1, 2, 5


def dot(a, b):
    return jnp.dot(a, b, preferred_element_type=F32)


def dot_first(a, b):
    return lax.dot_general(a, b, (((0,), (0,)), ((), ())), preferred_element_type=F32)


def dot_last(a, b):
    return lax.dot_general(a, b, (((1,), (1,)), ((), ())), preferred_element_type=F32)


def iota(shape, dim):
    return lax.broadcasted_iota(jnp.int32, shape, dim)


def hot(mask):
    return jnp.where(mask, 1.0, 0.0).astype(F32)


def lookup(table, index):
    return jnp.take_along_axis(table, index, axis=0, mode="promise_in_bounds")


def kernel(
    vol,
    lab,
    active,
    order,
    gain,
    bias,
    albedo,
    motion,
    conv_first,
    bias_first,
    conv_second,
    bias_second,
    aovs,
    denoised,
    volp,
    labi,
    labp,
    row_tmp,
    row_send,
    rowp,
    smat,
    kvec,
    tables,
    vs,
    gx,
    tc,
    qs,
    alpha_send,
    alpha_recv,
    front,
    front_send,
    front_recv,
    part,
    opaque,
    pair_send,
    pair_recv,
    chunk_send,
    chunk_recv,
    feat,
    edge,
    edge_recv,
    corner_recv,
    first_tmp,
    first_mat,
    second_tmp,
    second_mat,
    x_first,
    hidden,
    x_second,
    own_shift,
    rim_shift,
    second_shift,
    load_sem,
    halo_ssem,
    halo_rsem,
    alpha_ssem,
    alpha_rsem,
    front_ssem,
    front_rsem,
    pair_ssem,
    pair_rsem,
    chunk_ssem,
    chunk_rsem,
    rim_ssem,
    rim_rsem,
):
    me = lax.axis_index("depth")
    lat = lax.axis_index("lat")
    core = lax.rem(me, 2)
    chip = me // 2
    sibling = me + 1 - 2 * core
    ahead = lax.rem(me + 2, TILES)
    behind = lax.rem(me + TILES - 2, TILES)
    right = lax.rem(me + 1, TILES)
    left = lax.rem(me + TILES - 1, TILES)
    down = lax.rem(lat + 1, BANDS)
    up = lax.rem(lat + BANDS - 1, BANDS)
    not_first = hot(me > 0)
    not_last = hot(me < TILES - 1)
    not_top = hot(lat > 0)
    not_bottom = hot(lat < BANDS - 1)

    def remote(src, dst, ssem, rsem, device):
        return pltpu.make_async_remote_copy(
            src_ref=src,
            dst_ref=dst,
            send_sem=ssem,
            recv_sem=rsem,
            device_id=device,
            device_id_type=MESH,
        )

    load_vol = pltpu.make_async_copy(
        vol, volp.at[pl.ds(1, SLICES), :, pl.ds(LANES, COLS)], load_sem.at[0]
    )
    load_lab = pltpu.make_async_copy(lab, labi, load_sem.at[1])
    load_vol.start()
    load_lab.start()

    barrier = pltpu.get_barrier_semaphore()

    def greet(device):
        pl.semaphore_signal(barrier, inc=1, device_id=device, device_id_type=MESH)

    def greet_peer(i, carry):
        greet((lax.rem(me + i, TILES), lat))
        return carry

    lax.fori_loop(1, TILES, greet_peer, 0)
    for row in (up, down):
        for col in (left, me, right):
            greet((col, row))

    side = jnp.zeros((SLICES + 2, ROWS, LANES), BF16)
    volp[:, :, 0:LANES] = side
    volp[:, :, LANES + COLS :] = side
    labp[:, :, 0:LANES] = side[:SLICES]
    labp[:, :, LANES + COLS :] = side[:SLICES]
    rowp[:, :, 0:LANES] = side[0:2, 0:SLICES]
    rowp[:, :, LANES + COLS :] = side[0:2, 0:SLICES]
    feat[OWN:OWN_END] = jnp.zeros((ROWS * SLOTS, LANES), F32)

    class_of = iota((CLASSES, LANES), 0)
    sources = (
        [(gain, None), (bias, None)]
        + [(albedo, c) for c in range(3)]
        + [(motion, c) for c in range(2)]
    )
    for number, (ref, row) in enumerate(sources):
        table = jnp.zeros((CLASSES, LANES), F32)
        for k in range(CLASSES):
            value = ref[k] if row is None else ref[row, k]
            table = jnp.where(class_of == k, value, table)
        tables[number] = table * LOG2E if number < ALBEDO else table
    source_col = iota((3 * LANES, 2 * LANES), 0) - LANES
    target = iota((3 * LANES, 2 * LANES), 1)
    lane = lax.rem(target, LANES)
    for g in range(GROUPS):
        delta = source_col - lane + (STEP * me + g)
        smat[g] = jnp.where(
            target < LANES, hot(delta == 0), hot(delta == 1) - hot(delta == -1)
        ).astype(BF16)
    lane8 = iota((8, LANES), 1)
    for s in range(SLICES):
        factor = jnp.where(s < active[0, 0], -OPTICAL * LOG2E, 0.0).astype(F32)
        kvec[s, 1] = jnp.zeros((8, LANES), F32) + factor
        kvec[s, 0] = jnp.where(lane8 >= STEP * me + s // STEP, factor, 0.0)

    pl.semaphore_wait(barrier, TILES - 1 + 6)

    inner = pl.ds(LANES, COLS)
    halo = [
        remote(
            vol.at[SLICES - 1],
            volp.at[0, :, inner],
            halo_ssem.at[0],
            halo_rsem.at[0],
            (right, lat),
        ),
        remote(
            vol.at[0],
            volp.at[SLICES + 1, :, inner],
            halo_ssem.at[1],
            halo_rsem.at[1],
            (left, lat),
        ),
        remote(
            row_send.at[1],
            rowp.at[0, :, inner],
            halo_ssem.at[2],
            halo_rsem.at[2],
            (me, down),
        ),
        remote(
            row_send.at[0],
            rowp.at[1, :, inner],
            halo_ssem.at[3],
            halo_rsem.at[3],
            (me, up),
        ),
    ]
    halo[0].start()
    halo[1].start()
    load_vol.wait()
    for end in range(2):
        for s in range(SLICES):
            rows = volp[s + 1, 16 * end : 16 * end + 16, LANES : LANES + COLS].astype(F32)
            row_tmp[s : s + 1, :] = rows[15:16] if end else rows[0:1]
        row_send[end] = row_tmp[...].astype(BF16)
    halo[2].start()
    halo[3].start()

    load_lab.wait()

    def convert(s, carry):
        labp[s, :, LANES : LANES + COLS] = labi[s].astype(F32).astype(BF16)
        return carry

    lax.fori_loop(0, SLICES, convert, 0)

    def alpha_copy(j):
        return remote(
            alpha_send.at[j],
            alpha_recv.at[me],
            alpha_ssem.at[j],
            alpha_rsem.at[me],
            (j, lat),
        )

    def alpha_arrival(j):
        return remote(
            alpha_send.at[j],
            alpha_recv.at[j],
            alpha_ssem.at[j],
            alpha_rsem.at[j],
            (j, lat),
        )

    def window(j):
        return pl.ds(pl.multiple_of(j * LANES, LANES), 3 * LANES)

    def opacities(j, carry):
        through = [jnp.ones((8, LANES), F32) for _ in range(4)]
        edge_tile = jnp.minimum(j, 1)
        for g in range(GROUPS):
            first = STEP * g
            values = volp[1 + first : 1 + first + STEP, :, window(j)]
            marks = labp[first : first + STEP, :, window(j)]
            both = jnp.concatenate([values, marks], axis=0)
            moved = dot(both.reshape(2 * STEP * ROWS, 3 * LANES), smat[g, :, 0:LANES])
            classes = moved[STEP * ROWS :].astype(jnp.int32)
            moved = moved[: STEP * ROWS]
            vs[j, g, 1 : 1 + STEP, BODY] = moved.reshape(STEP, ROWS, LANES)
            qs[j, first : first + STEP] = classes.reshape(STEP, ROWS, LANES)
            slopes = dot(values.reshape(STEP * ROWS, 3 * LANES), smat[g, :, LANES : 2 * LANES])
            gx[j, first : first + STEP] = slopes.reshape(STEP, ROWS, LANES)
            for i in range(STEP):
                factor = kvec[first + i, edge_tile]
                for rb in range(4):
                    at = i * ROWS + rb * 8
                    q = classes[at : at + 8]
                    x = lookup(tables[GAIN], q) * moved[at : at + 8]
                    x = x + lookup(tables[BIAS], q)
                    t = jnp.exp2(factor * jnp.log(1.0 + jnp.exp2(x)))
                    tc[j, first + i, rb * 8 : rb * 8 + 8] = t
                    through[rb] = through[rb] * t
        opaque = 1.0 - jnp.concatenate(through, axis=0)
        alpha_send[j] = opaque.reshape(2, HALF, LANES).astype(BF16)

        @pl.when(j != me)
        def _():
            alpha_copy(j).start()

        return carry

    lax.fori_loop(0, TILES, opacities, 0)
    alpha_recv[me] = alpha_send[me]

    def boundary(first_tile):
        for g in range(GROUPS):
            lines = []
            for j in (first_tile, first_tile + 1):
                lines += [volp[STEP * g, :, window(j)], volp[STEP * g + STEP + 1, :, window(j)]]
                lines += [rowp[0, :, window(j)], rowp[1, :, window(j)]]
            both_tiles = dot(jnp.concatenate(lines, axis=0), smat[g, :, 0:LANES])
            for number in range(2):
                j = first_tile + number
                moved = both_tiles[number * 3 * ROWS : (number + 1) * 3 * ROWS]
                below, above = moved[0:ROWS], moved[ROWS : 2 * ROWS]
                vs[j, g, 0, BODY] = below * not_first if g == 0 else below
                vs[j, g, STEP + 1, BODY] = above * not_last if g == GROUPS - 1 else above
                over = moved[2 * ROWS : 2 * ROWS + SLICES] * not_top
                under = moved[2 * ROWS + SLICES :] * not_bottom
                for i in range(STEP):
                    s = STEP * g + i
                    vs[j, g, 1 + i, 7:8] = over[s : s + 1]
                    vs[j, g, 1 + i, 8 + ROWS : 9 + ROWS] = under[s : s + 1]

    def wait_alpha(i, carry):
        alpha_arrival(lax.rem(me + i, TILES)).wait_recv()
        return carry

    def distance_of(k):
        return jnp.where(lax.rem(k, 2) == 0, 4 - k // 2, k // 2 - 3)

    def front_copy(k):
        return remote(
            front_send.at[k],
            front_recv.at[me],
            front_ssem.at[k],
            front_rsem.at[me],
            (k, lat),
        )

    def front_arrival(k):
        return remote(
            front_send.at[k],
            front_recv.at[k],
            front_ssem.at[k],
            front_rsem.at[k],
            (k, lat),
        )

    def send_front(n, carry):
        other = lax.rem(chip - distance_of(n // 2) + CHIPS, CHIPS)
        k = 2 * other + jnp.where(lax.rem(n, 2) == 1, core, 1 - core)
        rank = jnp.int32(0)
        for j in range(TILES):
            rank = jnp.where(order[j] == k, j, rank)
        front_send[k] = jnp.round(front[rank] * UNIT).astype(jnp.int32).astype(jnp.int16)

        @pl.when(n < TILES - 1)
        def _():
            front_copy(k).start()

        return carry

    def exchange_fronts():
        lax.fori_loop(1, TILES, wait_alpha, 0)
        run = jnp.ones((2, HALF, LANES), F32)
        for j in range(TILES):
            front[j] = run
            run = run * (1.0 - alpha_recv[order[j]].astype(F32))
        opaque[...] = 1.0 - run
        lax.fori_loop(0, TILES, send_front, 0)
        front_recv[me] = front_send[me]

    def chunk_copy(k, p):
        return remote(
            chunk_send.at[k, p],
            chunk_recv.at[k, p],
            chunk_ssem.at[k, p],
            chunk_rsem.at[k, p],
            (jnp.where(lax.rem(k, 2) == 0, ahead, behind), lat),
        )

    def pair_copy(k):
        return remote(
            pair_send.at[k],
            pair_recv.at[k],
            pair_ssem.at[k],
            pair_rsem.at[k],
            (sibling, lat),
        )

    def render(tile, i_tile, h, rb):
        first = h * HALF + rb * 8
        r0 = pl.ds(pl.multiple_of(first, 8), 8)
        here = pl.ds(pl.multiple_of(first + 8, 8), 8)
        zero = jnp.zeros((8, LANES), F32)
        state = [zero] * SENT
        through = zero + 1.0
        for s in range(SLICES):
            g, i = s // STEP, s % STEP
            v = vs[tile, g, i + 1, here]
            below = vs[tile, g, i, here]
            above = vs[tile, g, i + 2, here]
            dx = gx[tile, s, r0]
            dy = vs[tile, g, i + 1, pl.ds(first + 9, 8)] - vs[tile, g, i + 1, pl.ds(first + 7, 8)]
            q = qs[tile, s, r0]
            dz = above - below
            inverse = lax.rsqrt(dx * dx + dy * dy + dz * dz + 4.0)
            later = through * tc[tile, s, r0]
            w = through - later
            through = later
            wn = w * inverse
            light = 0.288 * dx + 0.36 * dy + 0.384 * dz
            shaded = 0.4 * w + wn * jnp.maximum(light, 0.0)
            texture = 0.55 + 0.45 * jnp.tanh(below + above)
            plain = w * texture
            color = shaded * texture
            moving = w + (0.5 * w) * jnp.tanh(v)
            new = []
            tints = [lookup(tables[ALBEDO + c], q) for c in range(3)]
            new += [tint * color for tint in tints]
            new += [wn * dx, wn * dy, wn * dz]
            new += [tint * plain for tint in tints]
            new += [jnp.where(q == k, w, 0.0) for k in range(CLASSES - 1)]
            new += [lookup(tables[MOTION + c], q) * moving for c in range(2)]
            state = [a + b for a, b in zip(state, new)]
        final = state[0:16] + [a * (1.0 / MOTION_MAX) for a in state[16:18]]
        for c in range(SENT):
            part[i_tile, h, c, pl.ds(pl.multiple_of(rb * 8, 8), 8)] = final[c]

    def tile_of(i):
        kept = lax.rem(i, 2)
        tile_chip = lax.rem(chip + distance_of(i // 2) + CHIPS, CHIPS)
        return 2 * tile_chip + jnp.where(kept == 1, core, 1 - core)

    def scaled(i, p):
        h = p // (SENT // GROUP)
        channels = pl.ds(GROUP * lax.rem(p, SENT // GROUP), GROUP)
        image = part[i, h, channels].astype(BF16).astype(F32)
        return image * front_recv[tile_of(i), h].astype(jnp.int32).astype(F32)[None]

    def codes(i, p):
        return jnp.round(scaled(i, p)).astype(jnp.int32)

    def to_sibling(k):
        front_arrival(tile_of(2 * k)).wait_recv()

        def piece(p, carry):
            pair_send[k, p] = codes(2 * k, p).astype(jnp.int16)
            return carry

        lax.fori_loop(0, PIECES, piece, 0)
        pair_copy(k).start()

    def onward(k, p):
        if p == 0:
            pair_copy(k).wait_recv()
            front_arrival(tile_of(2 * k + 1)).wait_recv()
        total = codes(2 * k + 1, p) + pair_recv[k, p].astype(jnp.int32)
        if k >= 2:
            chunk_copy(k - 2, p).wait_recv()
            total = total + chunk_recv[k - 2, p].astype(jnp.int32)
        chunk_send[k, p] = total.astype(jnp.int16)
        chunk_copy(k, p).start()

    def tile_step(i, carry):
        tile = tile_of(i)

        @pl.when(lax.rem(i, 2) == 0)
        def _():
            boundary(2 * (tile // 2))


        def row_block(n, inner_carry):
            render(tile, i, n // 2, lax.rem(n, 2))
            return inner_carry

        lax.fori_loop(0, 4, row_block, 0)

        @pl.when(i == 1)
        def _():
            exchange_fronts()

        @pl.when(i == FRONT_AT)
        def _():
            def early_pair(k, inner_carry):
                to_sibling(k)
                return inner_carry

            lax.fori_loop(0, FRONT_AT // 2 + 1, early_pair, 0)

        @pl.when((i > FRONT_AT) & (lax.rem(i, 2) == 0))
        def _():
            to_sibling(i // 2)

        for at, pieces in ONWARD_AT.items():

            @pl.when(i == at)
            def _(pieces=pieces):
                for k, p in pieces:
                    onward(k, p)

        return carry

    for copy in halo:
        copy.wait()
    lax.fori_loop(0, TILES, tile_step, 0)

    onward(CHIPS - 2, 0)
    onward(CHIPS - 2, 1)

    turn = hot(iota((CHANNELS, CHANNELS), 0) == iota((CHANNELS, CHANNELS), 1)).astype(BF16)
    first_tmp[...] = jnp.zeros_like(first_tmp)
    second_tmp[...] = jnp.zeros_like(second_tmp)
    for dc in range(3):
        base = jnp.zeros((HIDDEN, 2 * LANES), F32)
        base2 = jnp.zeros((8, 3 * LANES), F32)
        for dr in range(3):
            first_tmp[:, 0:CHANNELS] = dot_first(conv_first[dr, dc], turn)
            wide = first_tmp[...]
            base = base + (pltpu.roll(wide, SLOTS * dr, 1) if dr else wide)
            second_tmp[0:3, 0:HIDDEN] = conv_second[dr, dc].astype(F32)
            wide = second_tmp[...]
            base2 = base2 + (pltpu.roll(wide, HIDDEN * dr, 1) if dr else wide)
        for i in range(8):
            moved = pltpu.roll(base, SLOTS * i, 1) if i else base
            first_mat[dc, i * HIDDEN : (i + 1) * HIDDEN, :] = moved.astype(BF16)
            moved = pltpu.roll(base2, HIDDEN * i, 1) if i else base2
            for c in range(3):
                second_mat[dc, c * 8 + i : c * 8 + i + 1, :] = moved[c : c + 1]

    n = iota((1, 6 * LANES), 1)
    tap = n // (2 * LANES) - 1
    spot = lax.rem(n, 2 * LANES)
    column = jnp.where(
        spot < LANES,
        spot + tap,
        jnp.where(
            spot == LANES, tap - 1, jnp.where(spot == LANES + 1, LANES + tap, -9)
        ),
    )
    own_shift[...] = hot(iota((LANES, 6 * LANES), 0) == column).astype(BF16)
    k16 = iota((16, 6 * LANES), 0)
    wanted = jnp.where(
        k16 < 2, k16 - 2, jnp.where((k16 == 10) | (k16 == 11), k16 + LANES - 10, -99)
    )
    rim_shift[...] = hot(wanted == column).astype(BF16)
    n = iota((1, 3 * LANES), 1)
    column = lax.rem(n, LANES) + n // LANES - 1
    source = jnp.where(column < 0, LANES, jnp.where(column == LANES, LANES + 1, column))
    second_shift[...] = hot(iota((2 * LANES, 3 * LANES), 0) == source).astype(BF16)
    x_first[:, OWN_END + OWN :, :] = jnp.zeros((3, FEATS - OWN_END - OWN, 2 * LANES), BF16)


    def keep(c, row, block):
        aovs[c, row : row + 8] = block
        start = OWN + row * SLOTS + c
        feat[pl.ds(start, 8, stride=SLOTS), :] = block.astype(BF16).astype(F32)

    pair_copy(CHIPS - 1).wait_recv()
    for h in range(2):
        blocks = []
        for piece in range(PIECES // 2):
            p = h * (PIECES // 2) + piece
            chunk_copy(CHIPS - 3, p).wait_recv()
            chunk_copy(CHIPS - 2, p).wait_recv()
            summed = pair_recv[CHIPS - 1, p].astype(jnp.int32)
            summed = summed + chunk_recv[CHIPS - 3, p].astype(jnp.int32)
            summed = summed + chunk_recv[CHIPS - 2, p].astype(jnp.int32)
            total = scaled(TILES - 1, p) + summed.astype(F32)
            blocks += [total[c] for c in range(GROUP)]
        for rb in range(2):
            row = h * HALF + rb * 8
            lines = [block[rb * 8 : rb * 8 + 8] * (1.0 / UNIT) for block in blocks]
            opacity = opaque[h, rb * 8 : rb * 8 + 8]
            covered = lines[9:16]
            last = opacity - sum(covered[1:], covered[0])
            moved = [line * MOTION_MAX for line in lines[16:18]]
            final = lines[0:3] + [opacity] + lines[3:9] + covered + [last] + moved
            for c in range(CHANNELS):
                keep(c, row, final[c])

    pick = iota((8, LANES), 0)
    at = iota((8, LANES), 1)
    chosen = (
        ((pick == 0) & (at == LANES - 2))
        | ((pick == 1) & (at == LANES - 1))
        | ((pick == 2) & (at == 0))
        | ((pick == 3) & (at == 1))
    )
    rim = [
        remote(
            feat.at[pl.ds(OWN, OWN)],
            feat.at[pl.ds(OWN_END, OWN)],
            rim_ssem.at[0],
            rim_rsem.at[0],
            (me, up),
        ),
        remote(
            feat.at[pl.ds(OWN_END - OWN, OWN)],
            feat.at[pl.ds(0, OWN)],
            rim_ssem.at[1],
            rim_rsem.at[1],
            (me, down),
        ),
    ]
    rim[0].start()
    rim[1].start()
    edge[...] = dot_last(hot(chosen).astype(BF16), feat[OWN:OWN_END].astype(BF16))
    top = pl.ds(0, LANES)
    bottom = pl.ds(ROWS * SLOTS - LANES, LANES)
    targets = [
        (edge, edge_recv.at[0], (right, lat)),
        (edge, edge_recv.at[1], (left, lat)),
        (edge.at[:, top], corner_recv.at[0], (right, up)),
        (edge.at[:, top], corner_recv.at[1], (left, up)),
        (edge.at[:, bottom], corner_recv.at[2], (right, down)),
        (edge.at[:, bottom], corner_recv.at[3], (left, down)),
    ]
    for number, (src, dst, device) in enumerate(targets):
        copy = remote(src, dst, rim_ssem.at[2 + number], rim_rsem.at[2 + number], device)
        copy.start()
        rim.append(copy)

    def put(start, end, values, add):
        for dc in range(3):
            for side in range(2):
                if add and dc == 1 and side == 0:
                    continue
                at = 2 * dc + side
                block = values[:, at * LANES : (at + 1) * LANES].astype(BF16)
                lanes = slice(side * LANES, (side + 1) * LANES)
                if add:
                    block = block + x_first[dc, start:end, lanes]
                x_first[dc, start:end, lanes] = block

    put(OWN, OWN_END, dot(feat[OWN:OWN_END].astype(BF16), own_shift[...]), False)
    for copy in rim:
        copy.wait()

    def both(first, second):
        return jnp.concatenate([first * not_first, second * not_last], axis=0).astype(BF16)

    put(OWN, OWN_END, dot_first(both(edge_recv[0], edge_recv[1]), rim_shift[...]), True)
    lower = dot_first(both(corner_recv[0], corner_recv[1]), rim_shift[...])
    upper = dot_first(both(corner_recv[2], corner_recv[3]), rim_shift[...])
    over = dot(feat[0:OWN].astype(BF16), own_shift[...])
    under = dot(feat[OWN_END : OWN_END + OWN].astype(BF16), own_shift[...])
    put(0, OWN, (over + upper[LANES - OWN :]) * not_top, False)
    put(OWN_END, OWN_END + OWN, (under + lower[0:OWN]) * not_bottom, False)

    eye = iota((HIDDEN, HIDDEN), 0) == iota((HIDDEN, HIDDEN), 1)
    bias_col = jnp.sum(jnp.where(eye, bias_first[...], 0.0), axis=1, keepdims=True)
    bias_all = jnp.concatenate([bias_col] * 8, axis=0)
    spot = iota((1, 2 * LANES), 1)
    inside = jnp.where(
        spot == LANES, not_first, jnp.where(spot == LANES + 1, not_last, 1.0)
    )
    row_of = iota((8 * HIDDEN, 1), 0) // HIDDEN
    for b in range(5):
        total = jnp.zeros((8 * HIDDEN, 2 * LANES), F32)
        for dc in range(3):
            x = x_first[dc, 8 * SLOTS * b : 8 * SLOTS * b + 2 * LANES, :]
            total = total + dot(first_mat[dc], x)
        total = jnp.maximum(total + bias_all, 0.0) * inside
        if b == 0:
            total = total * jnp.where(row_of == 0, not_top, 1.0)
        if b == 4:
            total = total * jnp.where(row_of == 1, not_bottom, 1.0)
        hidden[8 * HIDDEN * b : 8 * HIDDEN * (b + 1), :] = total.astype(BF16)

    moved = dot(hidden[...], second_shift[...])
    for dc in range(3):
        x_second[dc] = moved[:, dc * LANES : (dc + 1) * LANES].astype(BF16)
    for b in range(4):
        total = jnp.zeros((3 * 8, LANES), F32)
        for dc in range(3):
            x = x_second[dc, 8 * HIDDEN * b : 8 * HIDDEN * b + 10 * HIDDEN, :]
            total = total + dot(second_mat[dc][:, 0 : 10 * HIDDEN].astype(BF16), x)
        for c in range(3):
            rows = slice(8 * b, 8 * b + 8)
            color = aovs[c, rows] + total[8 * c : 8 * c + 8]
            denoised[c, rows] = color + bias_second[c]

    def sent(k, carry):
        other = lax.rem(me + k, TILES)
        alpha_copy(other).wait_send()
        front_copy(other).wait_send()
        return carry

    def passed(k, carry):
        for p in range(PIECES):
            chunk_copy(k, p).wait_send()
        return carry

    def paired(k, carry):
        pair_copy(k).wait_send()
        return carry

    lax.fori_loop(1, TILES, sent, 0)
    lax.fori_loop(0, CHIPS - 1, passed, 0)
    lax.fori_loop(0, CHIPS, paired, 0)


def per_device(
    volume,
    labels,
    active_slices,
    view_order,
    density_gain,
    density_bias,
    albedo_table,
    motion_table,
    conv_first,
    bias_first,
    conv_second,
    bias_second,
):
    smem = pl.BlockSpec(memory_space=pltpu.SMEM)
    vmem = pl.BlockSpec(memory_space=pltpu.VMEM)
    anywhere = pl.BlockSpec(memory_space=pl.ANY)
    cells = (TILES, SLICES, ROWS, LANES)
    tile = (TILES, 2, HALF, LANES)
    chunk = (CHANNELS, ROWS, LANES)
    pieces = (PIECES, GROUP, HALF, LANES)
    dma = pltpu.SemaphoreType.DMA
    return pl.pallas_call(
        kernel,
        out_shape=(
            jax.ShapeDtypeStruct(chunk, F32),
            jax.ShapeDtypeStruct((3, ROWS, LANES), F32),
        ),
        in_specs=[anywhere, anywhere] + [smem] * 6 + [vmem] * 3 + [smem],
        out_specs=(vmem, vmem),
        scratch_shapes=[
            pltpu.VMEM((SLICES + 2, ROWS, WIDE), BF16),
            pltpu.VMEM((SLICES, ROWS, COLS), jnp.int32),
            pltpu.VMEM((SLICES, ROWS, WIDE), BF16),
            pltpu.VMEM((SLICES, COLS), F32),
            pltpu.VMEM((2, SLICES, COLS), BF16),
            pltpu.VMEM((2, SLICES, WIDE), BF16),
            pltpu.VMEM((GROUPS, 3 * LANES, 2 * LANES), BF16),
            pltpu.VMEM((SLICES, 2, 8, LANES), F32),
            pltpu.VMEM((7, CLASSES, LANES), F32),
            pltpu.VMEM((TILES, GROUPS, STEP + 2, ROWS + 16, LANES), F32),
            pltpu.VMEM(cells, F32),
            pltpu.VMEM(cells, F32),
            pltpu.VMEM(cells, jnp.int32),
            pltpu.VMEM(tile, BF16),
            pltpu.VMEM(tile, BF16),
            pltpu.VMEM(tile, F32),
            pltpu.VMEM(tile, jnp.int16),
            pltpu.VMEM(tile, jnp.int16),
            pltpu.VMEM((TILES, 2, SENT, HALF, LANES), F32),
            pltpu.VMEM((2, HALF, LANES), F32),
            pltpu.VMEM((CHIPS,) + pieces, jnp.int16),
            pltpu.VMEM((CHIPS,) + pieces, jnp.int16),
            pltpu.VMEM((CHIPS - 1,) + pieces, jnp.int16),
            pltpu.VMEM((CHIPS - 1,) + pieces, jnp.int16),
            pltpu.VMEM((FEATS, LANES), F32),
            pltpu.VMEM((8, ROWS * SLOTS), F32),
            pltpu.VMEM((2, 8, ROWS * SLOTS), F32),
            pltpu.VMEM((4, 8, LANES), F32),
            pltpu.VMEM((HIDDEN, 2 * LANES), F32),
            pltpu.VMEM((3, 8 * HIDDEN, 2 * LANES), BF16),
            pltpu.VMEM((8, 3 * LANES), F32),
            pltpu.VMEM((3, 24, 3 * LANES), F32),
            pltpu.VMEM((3, FEATS, 2 * LANES), BF16),
            pltpu.VMEM((40 * HIDDEN, 2 * LANES), BF16),
            pltpu.VMEM((3, 40 * HIDDEN, LANES), BF16),
            pltpu.VMEM((LANES, 6 * LANES), BF16),
            pltpu.VMEM((16, 6 * LANES), BF16),
            pltpu.VMEM((2 * LANES, 3 * LANES), BF16),
            dma((2,)),
            dma((4,)),
            dma((4,)),
            dma((TILES,)),
            dma((TILES,)),
            dma((TILES,)),
            dma((TILES,)),
            dma((CHIPS,)),
            dma((CHIPS,)),
            dma((CHIPS - 1, PIECES)),
            dma((CHIPS - 1, PIECES)),
            dma((8,)),
            dma((8,)),
        ],
        compiler_params=pltpu.CompilerParams(
            collective_id=0, has_side_effects=True, vmem_limit_bytes=60 * 1024 * 1024
        ),
    )(
        volume,
        labels,
        active_slices,
        view_order,
        density_gain,
        density_bias,
        albedo_table,
        motion_table,
        jnp.swapaxes(conv_first, 2, 3),
        bias_first.reshape(1, HIDDEN),
        conv_second,
        bias_second,
    )


def solution(mesh):
    placed = (P("depth", "lat", None),) * 2 + (P("depth", "lat"),) + (P(),) * 9
    return jax.shard_map(
        per_device,
        mesh=mesh,
        in_specs=placed,
        out_specs=(P(None, "lat", "depth"), P(None, "lat", "depth")),
        check_vma=False,
    )
```
